512 devices in a mesh: attn: 64 (over z, y), ffn: 8 (over x, core).
Axes of the slice: x: 4, y: 8, z: 8, core: 2. Of those that a mesh axis runs over, the one named last changes fastest.
Arguments:
- residual: bfloat16 [512, 8192], P('attn', 'ffn'), may hold values from -12 to 12
- queries: bfloat16 [512, 8192], P('attn', 'ffn'), may hold values from -100 to 100
- cache_keys: bfloat16 [512, 8, 512, 128], P('attn', 'ffn'), may hold values from -4 to 4
- cache_values: bfloat16 [512, 8, 512, 128], P('attn', 'ffn'), may hold values from -6 to 6
- new_keys: bfloat16 [512, 8, 128], P('attn', 'ffn'), may hold values from -6 to 6
- new_values: bfloat16 [512, 8, 128], P('attn', 'ffn'), may hold values from -6 to 6
- lengths: int32 [512], P('attn'), may hold values from 1 to 512, as said below
- counts: int32 [64], P('attn'), may hold values from 1 to 8, 384 in all
- norm_gain: bfloat16 [8192], replicated, may hold values from 0.099609375 to 1.8984375
- gate_weight: bfloat16 [28672, 8192], P('attn', 'ffn'), may hold values from -0.0625 to 0.0625
- up_weight: bfloat16 [28672, 8192], P('attn', 'ffn'), may hold values from -0.0625 to 0.0625
- down_weight: bfloat16 [28672, 8192], P('attn', 'ffn'), may hold values from -0.09375 to 0.09375
Outputs:
- layer_out: bfloat16 [512, 8192], P('attn', 'ffn')
The draws below stay inside these ranges and needn't reach their ends.
Inputs may be any that keep to these rules, and one draw needn't show every extreme that they name: `lengths`: one slot holds exactly 512 cached positions. The counts sum to 384; some attention index has all 8 slots live.
All inputs are finite; a program needn't handle non-finite values. No bound on the sum of `counts` on one device may be relied on, other than what follows from the above.
Results may differ from the reference program's by a relative error of at most 0.017.
Values may be sent and summed in bfloat16 or wider, within the bound.
A program may use at most 64 MiB of HBM per device.

```python
import math
import jax
import jax.numpy as jnp
import numpy as np
from jax import lax

D = 8192
FF = 28672
QH = 64
KVH = 8
HD = 128
SLOTS = 8
CTX = 512
SLOTS_ALL = 512
ROWS = 384
N_ATTN = 64


def shared_keys(key):
    base_keys = jax.random.normal(key, (SLOTS * N_ATTN, KVH, CTX, HD), jnp.float32)
    return jnp.clip(base_keys, -4.0, 4.0)


def draw_cache_keys(key, part):
    base_keys = shared_keys(key)
    return base_keys.astype(jnp.bfloat16)


def draw_queries(key, part):
    key = jax.random.fold_in(key, 7)
    key_one = jax.random.fold_in(key, 0)
    slot_total = SLOTS * N_ATTN
    values_raw = 2.0 * jnp.clip(jax.random.normal(key_one, (slot_total, QH * HD), jnp.float32), -3.0, 3.0)
    return values_raw.astype(jnp.bfloat16)


def draw_residual(key, part):
    key = jax.random.fold_in(key, 3)
    key_one, key_two = jax.random.split(key, 2)
    slot_total = SLOTS * N_ATTN
    column = jnp.arange(D, dtype=jnp.float32) / D
    column_scale = 0.5 * jnp.power(3.0, column)[None, :]
    jitter = jax.random.uniform(key_two, (1, D), jnp.float32, 0.7, 1.3)
    values_raw = jnp.clip(jax.random.normal(key_one, (slot_total, D), jnp.float32), -6.0, 6.0)
    return (values_raw * column_scale * jitter).astype(jnp.bfloat16)


def draw_lengths(key, part):
    key = jax.random.fold_in(key, 9)
    key_one, key_two, key_three = jax.random.split(key, 3)
    upper_bound = jax.random.randint(key_one, (N_ATTN, 1), CTX // 8, CTX + 1)
    lengths_raw = jax.random.randint(key_two, (N_ATTN, SLOTS), 1, upper_bound + 1).reshape(SLOTS * N_ATTN)
    longest = jax.random.randint(key_three, (), 0, SLOTS * N_ATTN)
    lengths_raw = jnp.where(jnp.arange(SLOTS * N_ATTN) == longest, CTX, lengths_raw)
    return lengths_raw.astype(jnp.int32)


def strengthened(drawn, stream_key, source, target, shards_of, factor):
    def block_of(dim):
        return (jnp.arange(drawn.shape[dim]) // (drawn.shape[dim] // shards_of)).reshape((-1,) + (1,) * (drawn.ndim - 1 - dim))

    near = jax.random.permutation(stream_key, shards_of)[block_of(target)]
    second = (block_of(target) + shards_of // 2) % shards_of
    return jnp.where((block_of(source) == near) | (block_of(source) == second), factor * drawn, drawn)


def level_of(stream_key, dims, cuts, low, largest):
    loudness, own = 1.0, jax.random.fold_in(stream_key, 6)
    for dim, blocks in cuts:
        heights = jnp.exp(jax.random.uniform(jax.random.fold_in(own, dim), (blocks,), jnp.float32, low / len(cuts), largest / len(cuts)))
        loudness = loudness * jnp.repeat(heights, dims[dim] // blocks).reshape([-1 if axis == dim else 1 for axis in range(len(dims))])
    return loudness


def split_up(number_of, total, most, lean):
    loads = [(1 << 20) // math.isqrt(grade ** lean) + 1 for grade in range(2, number_of + 1)]
    rest, given = total - most - (number_of - 1), [1] * (number_of - 1)
    while rest > 0:
        movable = [i for i in range(number_of - 1) if given[i] < most]
        whole, remaining = sum([loads[i] for i in movable]), rest
        for i in movable:
            extra = min(most - given[i], max(1, remaining * loads[i] // whole), rest)
            given[i] = given[i] + extra
            rest = rest - extra
    return np.array([most] + given)


def uneven_parts(rng, number_of, total, reach, slope):
    if number_of == 2:
        one = jax.random.randint(rng, (), max(1, total - reach), min(reach, total - 1) + 1)
        return jnp.stack([one, total - one])
    sizes = jnp.asarray(split_up(number_of, total, reach, slope), jnp.int32)
    pairs = (number_of - 1) // 2
    giver, sink = sizes[1:1 + 2 * pairs:2], sizes[2:2 + 2 * pairs:2]
    room = jnp.minimum(giver - 1, reach - sink)
    passed = jax.random.randint(jax.random.fold_in(rng, 1), (pairs,), 0, 1 << 20) % (room + 1)
    sizes = sizes.at[1:1 + 2 * pairs:2].set(giver - passed).at[2:2 + 2 * pairs:2].set(sink + passed)
    return sizes[jax.random.permutation(jax.random.fold_in(rng, 2), number_of)]


def scatter_about(stream_key, extent, deviation, reach, cuts=(), kind=jnp.bfloat16):
    entries = deviation * jax.random.normal(stream_key, extent, jnp.float32)
    if cuts:
        entries = entries * level_of(stream_key, extent, cuts, -0.22, 0.18)
    return jnp.clip(entries, -reach, reach).astype(kind)


def noise_with(stream_key, dims, spread, bound, pieces, heavy, held_as=jnp.bfloat16):
    drawn = spread * jax.random.normal(stream_key, dims, jnp.float32)
    if pieces:
        drawn = drawn * level_of(stream_key, dims, pieces, -0.22, 0.18)
    return jnp.clip(strengthened(drawn, jax.random.fold_in(stream_key, 3), *heavy), -bound, bound).astype(held_as)


def setup_inputs(seed: int = 0) -> dict:
    seeds = jax.random.split(jax.random.key(seed), 13)
    return {
        "residual": draw_residual(jax.random.fold_in(seeds[12], 71), 0),
        "queries": draw_queries(jax.random.fold_in(seeds[12], 71), 0),
        "cache_keys": draw_cache_keys(jax.random.fold_in(seeds[12], 71), 0),
        "cache_values": scatter_about(seeds[3], (SLOTS_ALL, KVH, CTX, HD), 1.0, 6.0, ((0, 64), (1, 8))),
        "new_keys": scatter_about(seeds[4], (SLOTS_ALL, KVH, HD), 1.0, 6.0, ((0, 64), (1, 8))),
        "new_values": scatter_about(seeds[5], (SLOTS_ALL, KVH, HD), 1.0, 6.0, ((0, 64), (1, 8))),
        "lengths": draw_lengths(jax.random.fold_in(seeds[12], 71), 0),
        "counts": uneven_parts(seeds[7], N_ATTN, ROWS, SLOTS, 1).astype(jnp.int32),
        "norm_gain": jnp.clip(1.0 + 0.18 * jax.random.normal(seeds[8], (D,), jnp.float32), 0.099609375, 1.8984375).astype(jnp.bfloat16),
        "gate_weight": scatter_about(seeds[9], (FF, D), D ** -0.5, 0.0625, ((0, 64), (1, 8))),
        "up_weight": scatter_about(seeds[10], (FF, D), D ** -0.5, 0.0625, ((0, 64), (1, 8))),
        "down_weight": noise_with(seeds[11], (FF, D), FF ** -0.5, 0.09375, ((0, 64), (1, 8)), (0, 1, 64, 4.0)),
    }


epsilon = 1e-05

def reference(residual, queries, cache_keys, cache_values, new_keys, new_values, lengths, counts, norm_gain, gate_weight, up_weight, down_weight):
    head_group = QH // KVH
    score_scale = 1.0 / HD ** 0.5
    positions = jnp.arange(CTX, dtype=jnp.int32)

    def one_slot(slot_data):
        query_row, slot_keys, slot_values, fresh_key, fresh_value, length = slot_data
        query_f32 = query_row.reshape(KVH, head_group, HD).astype(jnp.float32)
        scores = jnp.einsum('gqd,gpd->gqp', query_f32, slot_keys.astype(jnp.float32)) * score_scale
        scores = jnp.where(positions[None, None, :] < length, scores, -1e+30)
        own_score = jnp.einsum('gqd,gd->gq', query_f32, fresh_key.astype(jnp.float32)) * score_scale
        row_max = jnp.maximum(lax.optimization_barrier(jnp.max(scores, axis=-1)), own_score)
        key_weights = jnp.exp(scores - row_max[..., None])
        own_weight = jnp.exp(own_score - row_max)
        denominator = lax.optimization_barrier(jnp.sum(key_weights, axis=-1)) + own_weight
        key_probs = (key_weights / denominator[..., None]).astype(jnp.bfloat16)
        own_prob = (own_weight / denominator).astype(jnp.bfloat16)
        mixed = jnp.einsum('gqp,gpd->gqd', key_probs.astype(jnp.float32), slot_values.astype(jnp.float32))
        mixed = mixed + own_prob.astype(jnp.float32)[..., None] * fresh_value.astype(jnp.float32)[:, None, :]
        return mixed.reshape(QH * HD).astype(jnp.bfloat16)
    attention = lax.map(one_slot, (queries, cache_keys, cache_values, new_keys, new_values, lengths))
    attention = lax.optimization_barrier(attention)
    hidden = (residual.astype(jnp.float32) + attention.astype(jnp.float32)).astype(jnp.bfloat16)
    hidden_f32 = hidden.astype(jnp.float32)
    mean_square = lax.optimization_barrier(jnp.mean(hidden_f32 * hidden_f32, axis=-1, keepdims=True))
    normed = (hidden_f32 * lax.rsqrt(mean_square + epsilon) * norm_gain.astype(jnp.float32)).astype(jnp.bfloat16)
    gate = jnp.dot(normed, gate_weight.T, preferred_element_type=jnp.float32)
    up_part = jnp.dot(normed, up_weight.T, preferred_element_type=jnp.float32)
    activated = (jax.nn.silu(gate) * up_part).astype(jnp.bfloat16)
    ffn_out = jnp.dot(activated, down_weight, preferred_element_type=jnp.float32)
    slot_total = residual.shape[0]
    slot_index = jnp.arange(slot_total, dtype=jnp.int32)
    is_live = slot_index % SLOTS < jnp.repeat(counts, SLOTS)
    result = jnp.where(is_live[:, None], hidden_f32 + ffn_out, 0.0)
    return result.astype(jnp.bfloat16)
```

```python
import jax
import jax.numpy as jnp
from jax import lax
from jax.experimental import pallas as pl
from jax.experimental.pallas import tpu as pltpu
from jax.sharding import PartitionSpec as P

D = 8192


epsilon = 1e-05


def attend(queries, cache_keys, cache_values, new_keys, new_values, lengths):
    slot_count = queries.shape[0]
    kv_dev = cache_keys.shape[1]
    ctx_len = cache_keys.shape[2]
    head_dim = cache_keys.shape[3]
    head_group = queries.shape[1] // (kv_dev * head_dim)
    score_scale = 1.0 / head_dim**0.5
    query_heads = queries.reshape(slot_count, kv_dev, head_group, head_dim)
    scores = (
        jnp.einsum("rgqd,rgpd->rgqp", query_heads, cache_keys, preferred_element_type=jnp.float32)
        * score_scale
    )
    positions = jnp.arange(ctx_len, dtype=jnp.int32)
    allowed = positions[None, None, None, :] < lengths[:, None, None, None]
    scores = jnp.where(allowed, scores, -1e30)
    own_score = (
        jnp.einsum("rgqd,rgd->rgq", query_heads, new_keys, preferred_element_type=jnp.float32)
        * score_scale
    )
    row_max = jnp.maximum(jnp.max(scores, axis=-1), own_score)
    key_weights = jnp.exp(scores - row_max[..., None])
    own_weight = jnp.exp(own_score - row_max)
    denominator = jnp.sum(key_weights, axis=-1) + own_weight
    key_probs = (key_weights / denominator[..., None]).astype(jnp.bfloat16)
    own_prob = (own_weight / denominator).astype(jnp.bfloat16)
    mixed = jnp.einsum(
        "rgqp,rgpd->rgqd", key_probs, cache_values, preferred_element_type=jnp.float32
    )
    mixed = (
        mixed
        + own_prob.astype(jnp.float32)[..., None] * new_values.astype(jnp.float32)[:, :, None, :]
    )
    return mixed.reshape(slot_count, kv_dev * head_group * head_dim).astype(jnp.bfloat16)


MESH = pl.DeviceIdType.MESH
N = 8
NX = 4
HALF = 512
UNITS = 448
MAIN = 384
TILES = ((0, 256), (256, 256), (512, 256), (768, 128))


def transposed_dot(rows, weight):
    return lax.dot_general(rows, weight, (((1,), (1,)), ((), ())), preferred_element_type=jnp.float32)


def kernel(
    hidden_ref,
    gain_ref,
    gate_hbm,
    up_hbm,
    down_hbm,
    out_ref,
    gu,
    down,
    ga,
    gb,
    xs,
    ssb,
    pair_out,
    pair_in,
    pair_ss,
    own,
    x_out,
    x_in,
    x_ss_out,
    x_ss_in,
    act,
    da,
    db,
    ra,
    rb,
    d2a,
    d2b,
    r2a,
    r2b,
    wsem,
    g1s,
    g1r,
    g2s,
    g2r,
    ps,
    pr,
    xsd,
    xrv,
    acs,
    acr,
    r1s,
    r1r,
    r2s,
    r2r,
):
    attn = lax.axis_index("attn")
    ffn = lax.axis_index("ffn")
    z, y = lax.div(attn, N), lax.rem(attn, N)
    x, c = lax.div(ffn, 2), lax.rem(ffn, 2)

    def at(zz, yy, xx, cc):
        return (zz * N + yy, xx * 2 + cc)

    def past(i, k, n):
        return lax.rem(i + k, n)

    loads = [
        pltpu.make_async_copy(gate_hbm, gu.at[pl.ds(0, UNITS)], wsem.at[0]),
        pltpu.make_async_copy(up_hbm.at[pl.ds(MAIN, UNITS - MAIN)], gu.at[pl.ds(UNITS, UNITS - MAIN)], wsem.at[1]),
        pltpu.make_async_copy(up_hbm.at[pl.ds(0, MAIN)], gu.at[pl.ds(512, MAIN)], wsem.at[2]),
        pltpu.make_async_copy(down_hbm, down, wsem.at[3]),
    ]
    for load in loads:
        load.start()

    barrier = pltpu.get_barrier_semaphore()
    partners = [at(past(z, k, N), y, x, c) for k in range(1, N)]
    partners += [at(z, past(y, k, N), x, c) for k in range(1, N)]
    partners += [at(z, y, past(x, k // 2, NX), past(c, k % 2, 2)) for k in range(1, 2 * NX)]
    for partner in partners:
        pl.semaphore_signal(barrier, inc=1, device_id=partner, device_id_type=MESH)
    pl.semaphore_wait(barrier, len(partners))

    sent = []

    def send(source, target, send_sem, recv_sem, device):
        copy = pltpu.make_async_remote_copy(
            src_ref=source, dst_ref=target, send_sem=send_sem, recv_sem=recv_sem, device_id=device, device_id_type=MESH
        )
        copy.start()
        sent.append(copy)
        return copy

    ga[z, y] = hidden_ref[:, :HALF]
    gb[y, z] = hidden_ref[:, HALF:]
    first = []
    for k in range(1, N):
        first.append(send(ga.at[z, y], ga.at[z, y], g1s.at[0, k], g1r.at[0, k], at(z, past(y, k, N), x, c)))
        first.append(send(gb.at[y, z], gb.at[y, z], g1s.at[1, k], g1r.at[1, k], at(past(z, k, N), y, x, c)))
    for copy in first:
        copy.wait_recv()
    second = []
    for k in range(1, N):
        second.append(send(ga.at[z], ga.at[z], g2s.at[0, k], g2r.at[0, k], at(past(z, k, N), y, x, c)))
        second.append(send(gb.at[y], gb.at[y], g2s.at[1, k], g2r.at[1, k], at(z, past(y, k, N), x, c)))
    for copy in second:
        copy.wait_recv()

    gain_a = gain_ref[:, :HALF]
    gain_b = gain_ref[:, HALF:]
    lane = lax.broadcasted_iota(jnp.int32, (64, 128), 1)
    row = lax.broadcasted_iota(jnp.int32, (64, 128), 0)
    diagonal = lane == row

    def scale(zz, carry):
        place = lax.rem(zz, 2) * 4 + lax.div(zz, 2)
        part_a = ga[zz].astype(jnp.float32).reshape(64, HALF)
        part_b = gb[:, zz].astype(jnp.float32).reshape(64, HALF)
        squares = jnp.sum(part_a * part_a + part_b * part_b, axis=1, keepdims=True)
        ssb[place] = jnp.sum(jnp.where(diagonal, squares, 0.0), axis=0, keepdims=True)
        xs[place, :, :HALF] = (part_a * gain_a).astype(jnp.bfloat16)
        xs[place, :, HALF:] = (part_b * gain_b).astype(jnp.bfloat16)
        return carry

    lax.fori_loop(0, N, scale, 0)
    for load in loads:
        load.wait()

    rows = xs[pl.ds((1 - c) * 4, 4)].reshape(256, 1024)
    for start, width in TILES:
        block = transposed_dot(rows, gu[start : start + width, :])
        pair_out[:, :, start : start + width] = block.astype(jnp.bfloat16).reshape(4, 64, width)
    other = at(z, y, x, 1 - c)
    pair = [
        send(pair_out, pair_in, ps.at[0], pr.at[0], other),
        send(ssb.at[pl.ds((1 - c) * 4, 4)], pair_ss, ps.at[1], pr.at[1], other),
    ]
    rows = xs[pl.ds(c * 4, 4)].reshape(256, 1024)
    for start, width in TILES:
        own[:, :, start : start + width] = transposed_dot(rows, gu[start : start + width, :]).reshape(4, 64, width)
    for copy in pair:
        copy.wait_recv()
    across = []
    for k in range(1, NX):
        xx = past(x, k, NX)
        x_out[k] = (own[xx] + pair_in[xx].astype(jnp.float32)).astype(jnp.bfloat16)
        x_ss_out[k] = ssb[c * 4 + xx] + pair_ss[xx]
        across.append(send(x_out.at[k], x_in.at[k], xsd.at[0, k], xrv.at[0, k], at(z, y, xx, c)))
        across.append(send(x_ss_out.at[k], x_ss_in.at[k], xsd.at[1, k], xrv.at[1, k], at(z, y, xx, c)))
    total = own[x] + pair_in[x].astype(jnp.float32)
    squares = ssb[c * 4 + x] + pair_ss[x]
    for copy in across:
        copy.wait_recv()
    for k in range(1, NX):
        total = total + x_in[k].astype(jnp.float32)
        squares = squares + x_ss_in[k]
    mean_square = jnp.sum(jnp.where(diagonal, squares, 0.0), axis=1, keepdims=True) / D
    total = total * lax.rsqrt(mean_square + epsilon)
    gate = total[:, :512]
    silu = gate / (1.0 + jnp.exp(-gate))
    act[ffn, :, :MAIN] = (silu[:, :MAIN] * total[:, 512:]).astype(jnp.bfloat16)
    tail = silu[:, MAIN:] * pltpu.roll(total[:, MAIN:512], 64, 1)
    act[ffn, :, MAIN:] = tail[:, : UNITS - MAIN].astype(jnp.bfloat16)
    spread = []
    for k in range(1, 2 * NX):
        device = at(z, y, past(x, k // 2, NX), past(c, k % 2, 2))
        spread.append(send(act.at[ffn], act.at[ffn], acs.at[k], acr.at[k], device))
    for copy in spread:
        copy.wait_recv()

    ones = []
    for half, (buffer, back) in enumerate(((da, ra), (db, rb))):
        for m in range(2):
            rows = act[4 * m : 4 * m + 4].reshape(256, UNITS)
            for start in (0, 256):
                block = jnp.dot(
                    rows, down[:, half * HALF + start : half * HALF + start + 256], preferred_element_type=jnp.float32
                ).astype(jnp.bfloat16)
                block = block.reshape(4, N, 8, 256)
                if half == 0:
                    buffer[4 * m : 4 * m + 4, :, :, start : start + 256] = block
                else:
                    for i in range(4):
                        buffer[:, 4 * m + i, :, start : start + 256] = block[i]
        for k in range(1, N):
            if half == 0:
                there, device = past(z, k, N), at(past(z, k, N), y, x, c)
            else:
                there, device = past(y, k, N), at(z, past(y, k, N), x, c)
            ones.append(send(buffer.at[there], back.at[k], r1s.at[half, k], r1r.at[half, k], device))
    twos = []
    for half, (buffer, back, onward, last) in enumerate(((da, ra, d2a, r2a), (db, rb, d2b, r2b))):
        here = z if half == 0 else y
        for copy in ones[half * 7 : half * 7 + 7]:
            copy.wait_recv()
        added = buffer[here].astype(jnp.float32)
        for k in range(1, N):
            added = added + back[k].astype(jnp.float32)
        onward[...] = added.astype(jnp.bfloat16)
        for k in range(1, N):
            if half == 0:
                there, device = past(y, k, N), at(z, past(y, k, N), x, c)
            else:
                there, device = past(z, k, N), at(past(z, k, N), y, x, c)
            twos.append(send(onward.at[there], last.at[k], r2s.at[half, k], r2r.at[half, k], device))
    for half, (onward, last) in enumerate(((d2a, r2a), (d2b, r2b))):
        here = y if half == 0 else z
        for copy in twos[half * 7 : half * 7 + 7]:
            copy.wait_recv()
        added = onward[here].astype(jnp.float32)
        for k in range(1, N):
            added = added + last[k].astype(jnp.float32)
        out_ref[:, half * HALF : half * HALF + HALF] = added
    for copy in sent:
        copy.wait_send()


def feed_forward(hidden, gain, gate_weight, up_weight, down_weight):
    bf, f32 = jnp.bfloat16, jnp.float32
    dma = pltpu.SemaphoreType.DMA
    vmem = pltpu.VMEM
    return pl.pallas_call(
        kernel,
        out_shape=jax.ShapeDtypeStruct((8, 1024), f32),
        in_specs=[pl.BlockSpec(memory_space=vmem)] * 2 + [pl.BlockSpec(memory_space=pl.ANY)] * 3,
        out_specs=pl.BlockSpec(memory_space=vmem),
        scratch_shapes=[
            vmem((896, 1024), bf),
            vmem((UNITS, 1024), bf),
            vmem((N, N, 8, HALF), bf),
            vmem((N, N, 8, HALF), bf),
            vmem((N, 64, 1024), bf),
            vmem((N, 1, 128), f32),
            vmem((4, 64, 896), bf),
            vmem((4, 64, 896), bf),
            vmem((4, 1, 128), f32),
            vmem((4, 64, 896), f32),
            vmem((NX, 64, 896), bf),
            vmem((NX, 64, 896), bf),
            vmem((NX, 1, 128), f32),
            vmem((NX, 1, 128), f32),
            vmem((2 * NX, 64, UNITS), bf),
            vmem((N, N, 8, HALF), bf),
            vmem((N, N, 8, HALF), bf),
            vmem((N, N, 8, HALF), bf),
            vmem((N, N, 8, HALF), bf),
            vmem((N, 8, HALF), bf),
            vmem((N, 8, HALF), bf),
            vmem((N, 8, HALF), bf),
            vmem((N, 8, HALF), bf),
            dma((4,)),
            dma((2, N)),
            dma((2, N)),
            dma((2, N)),
            dma((2, N)),
            dma((2,)),
            dma((2,)),
            dma((2, NX)),
            dma((2, NX)),
            dma((2 * NX,)),
            dma((2 * NX,)),
            dma((2, N)),
            dma((2, N)),
            dma((2, N)),
            dma((2, N)),
        ],
        compiler_params=pltpu.CompilerParams(
            collective_id=0, has_side_effects=True, vmem_limit_bytes=40 * 1024 * 1024
        ),
        cost_estimate=pl.CostEstimate(flops=1_400_000_000, bytes_accessed=3_000_000, transcendentals=0),
        name="feed_forward",
    )(hidden, gain, gate_weight, up_weight, down_weight)


def on_device(
    residual,
    queries,
    cache_keys,
    cache_values,
    new_keys,
    new_values,
    lengths,
    counts,
    norm_gain,
    gate_weight,
    up_weight,
    down_weight,
):
    slot_count = residual.shape[0]
    width_dev = residual.shape[1]
    attention = attend(queries, cache_keys, cache_values, new_keys, new_values, lengths)
    hidden = (residual.astype(jnp.float32) + attention.astype(jnp.float32)).astype(jnp.bfloat16)
    gain_block = lax.dynamic_slice_in_dim(norm_gain, lax.axis_index("ffn") * width_dev, width_dev)
    gain = gain_block.astype(jnp.float32)[None, :]
    ffn_out = feed_forward(hidden, gain, gate_weight, up_weight, down_weight)
    is_live = jnp.arange(slot_count, dtype=jnp.int32) < counts[0]
    result = jnp.where(is_live[:, None], hidden.astype(jnp.float32) + ffn_out, 0.0)
    return result.astype(jnp.bfloat16)


def solution(mesh):
    return jax.shard_map(
        on_device,
        mesh=mesh,
        in_specs=(
            P("attn", "ffn"),
            P("attn", "ffn"),
            P("attn", "ffn", None, None),
            P("attn", "ffn", None, None),
            P("attn", "ffn", None),
            P("attn", "ffn", None),
            P("attn"),
            P("attn"),
            P(),
            P("attn", "ffn"),
            P("attn", "ffn"),
            P("attn", "ffn"),
        ),
        out_specs=P("attn", "ffn"),
        check_vma=False,
    )
```

```python
import jax
import jax.numpy as jnp
from jax import lax
from jax.experimental import pallas as pl
from jax.experimental.pallas import tpu as pltpu
from jax.sharding import PartitionSpec as P

D = 8192


epsilon = 1e-05


def attend(queries, cache_keys, cache_values, new_keys, new_values, lengths):
    slot_count = queries.shape[0]
    kv_dev = cache_keys.shape[1]
    ctx_len = cache_keys.shape[2]
    head_dim = cache_keys.shape[3]
    head_group = queries.shape[1] // (kv_dev * head_dim)
    score_scale = 1.0 / head_dim**0.5
    query_heads = queries.reshape(slot_count, kv_dev, head_group, head_dim)
    scores = (
        jnp.einsum("rgqd,rgpd->rgqp", query_heads, cache_keys, preferred_element_type=jnp.float32)
        * score_scale
    )
    positions = jnp.arange(ctx_len, dtype=jnp.int32)
    allowed = positions[None, None, None, :] < lengths[:, None, None, None]
    scores = jnp.where(allowed, scores, -1e30)
    own_score = (
        jnp.einsum("rgqd,rgd->rgq", query_heads, new_keys, preferred_element_type=jnp.float32)
        * score_scale
    )
    row_max = jnp.maximum(jnp.max(scores, axis=-1), own_score)
    key_weights = jnp.exp(scores - row_max[..., None])
    own_weight = jnp.exp(own_score - row_max)
    denominator = jnp.sum(key_weights, axis=-1) + own_weight
    key_probs = (key_weights / denominator[..., None]).astype(jnp.bfloat16)
    own_prob = (own_weight / denominator).astype(jnp.bfloat16)
    mixed = jnp.einsum(
        "rgqp,rgpd->rgqd", key_probs, cache_values, preferred_element_type=jnp.float32
    )
    mixed = (
        mixed
        + own_prob.astype(jnp.float32)[..., None] * new_values.astype(jnp.float32)[:, :, None, :]
    )
    return mixed.reshape(slot_count, kv_dev * head_group * head_dim).astype(jnp.bfloat16)


MESH = pl.DeviceIdType.MESH
N = 8
NX = 4
PARTS = 2
QUARTER = 256
UNITS = 448
MAIN = 384
TILES = ((0, 256), (256, 256), (512, 256), (768, 128))


def transposed_dot(rows, weight):
    return lax.dot_general(rows, weight, (((1,), (1,)), ((), ())), preferred_element_type=jnp.float32)


def exchange(low, high):
    axis = low.ndim - 2
    upper = lax.broadcasted_iota(jnp.int32, low.shape, axis) < 4
    return jnp.where(upper, low, pltpu.roll(high, 4, axis)), jnp.where(upper, pltpu.roll(low, 4, axis), high)


def kernel(
    hidden_ref,
    gain_ref,
    gate_hbm,
    up_hbm,
    down_hbm,
    out_ref,
    gu,
    down,
    ga,
    gb,
    xs,
    ssb,
    pair_out,
    pair_in,
    pair_ss,
    own,
    x_out,
    x_in,
    x_ss_out,
    x_ss_in,
    act,
    da,
    db,
    ra,
    rb,
    d2a,
    d2b,
    r2a,
    r2b,
    wsem,
    g1s,
    g1r,
    g2s,
    g2r,
    ps,
    pr,
    xsd,
    xrv,
    acs,
    acr,
    fws,
    fwr,
    r1s,
    r1r,
    r2s,
    r2r,
):
    attn = lax.axis_index("attn")
    ffn = lax.axis_index("ffn")
    z, y = lax.div(attn, N), lax.rem(attn, N)
    x, c = lax.div(ffn, 2), lax.rem(ffn, 2)

    def at(zz, yy, xx, cc):
        return (zz * N + yy, xx * 2 + cc)

    def past(i, k, n):
        return lax.rem(i + k, n)

    loads = [
        pltpu.make_async_copy(gate_hbm, gu.at[pl.ds(0, UNITS)], wsem.at[0]),
        pltpu.make_async_copy(up_hbm.at[pl.ds(MAIN, UNITS - MAIN)], gu.at[pl.ds(UNITS, UNITS - MAIN)], wsem.at[1]),
        pltpu.make_async_copy(up_hbm.at[pl.ds(0, MAIN)], gu.at[pl.ds(512, MAIN)], wsem.at[2]),
        pltpu.make_async_copy(down_hbm, down, wsem.at[3]),
    ]
    for load in loads:
        load.start()

    barrier = pltpu.get_barrier_semaphore()
    partners = [at(past(z, k, N), y, x, c) for k in range(1, N)]
    partners += [at(z, past(y, k, N), x, c) for k in range(1, N)]
    partners += [at(z, y, past(x, k, NX), c) for k in range(1, NX)]
    partners += [at(z, y, x, 1 - c)]
    for partner in partners:
        pl.semaphore_signal(barrier, inc=1, device_id=partner, device_id_type=MESH)
    pl.semaphore_wait(barrier, len(partners))

    sent = []

    def send(source, target, send_sem, recv_sem, device):
        copy = pltpu.make_async_remote_copy(
            src_ref=source, dst_ref=target, send_sem=send_sem, recv_sem=recv_sem, device_id=device, device_id_type=MESH
        )
        copy.start()
        sent.append(copy)
        return copy

    other = at(z, y, x, 1 - c)
    lane = lax.broadcasted_iota(jnp.int32, (32, 128), 1)
    row = lax.broadcasted_iota(jnp.int32, (32, 128), 0)
    diagonal = lane == row

    def along(first_is_z, k):
        if first_is_z:
            return past(z, k, N), at(past(z, k, N), y, x, c)
        return past(y, k, N), at(z, past(y, k, N), x, c)

    wide = hidden_ref[...].astype(jnp.float32)
    for buffer, start, one, two in ((ga, 0, z, y), (gb, 512, y, z)):
        blocks = exchange(wide[:, start : start + QUARTER], wide[:, start + QUARTER : start + 512])
        for p in range(PARTS):
            buffer[p, one, two] = blocks[p].astype(jnp.bfloat16)

    def gather_first(p):
        copies = []
        for k in range(1, N):
            copies.append(send(ga.at[p, z, y], ga.at[p, z, y], g1s.at[p, 0, k], g1r.at[p, 0, k], along(False, k)[1]))
            copies.append(send(gb.at[p, y, z], gb.at[p, y, z], g1s.at[p, 1, k], g1r.at[p, 1, k], along(True, k)[1]))
        return copies

    def gather_second(p, before):
        for copy in before:
            copy.wait_recv()
        copies = []
        for k in range(1, N):
            copies.append(send(ga.at[p, z], ga.at[p, z], g2s.at[p, 0, k], g2r.at[p, 0, k], along(True, k)[1]))
            copies.append(send(gb.at[p, y], gb.at[p, y], g2s.at[p, 1, k], g2r.at[p, 1, k], along(False, k)[1]))
        return copies

    def rows_of(packed):
        packed = packed.astype(jnp.float32).reshape(4, 2, 8, QUARTER)
        low, high = exchange(packed[:, 0], packed[:, 1])
        return [low.reshape(32, QUARTER), high.reshape(32, QUARTER)]

    def multiply(p, before):
        for copy in before:
            copy.wait_recv()

        def scale(zz, carry):
            place = lax.rem(zz, 2) * 4 + lax.div(zz, 2)
            quarters = rows_of(ga[p, zz]) + rows_of(gb[p, :, zz])
            squares = quarters[0] * quarters[0]
            for part in quarters[1:]:
                squares = squares + part * part
            squares = jnp.sum(squares, axis=1, keepdims=True)
            ssb[p, place] = jnp.sum(jnp.where(diagonal, squares, 0.0), axis=0, keepdims=True)
            for i, part in enumerate(quarters):
                lanes = slice(i * QUARTER, (i + 1) * QUARTER)
                xs[p, place, :, lanes] = (part * gain_ref[:, lanes]).astype(jnp.bfloat16)
            return carry

        lax.fori_loop(0, N, scale, 0)
        if p == 0:
            for load in loads:
                load.wait()
        rows = xs[p, pl.ds((1 - c) * 4, 4)].reshape(128, 1024)
        for start, width in TILES:
            block = transposed_dot(rows, gu[start : start + width, :])
            pair_out[p, :, :, start : start + width] = block.astype(jnp.bfloat16).reshape(4, 32, width)
        pair = [
            send(pair_out.at[p], pair_in.at[p], ps.at[p, 0], pr.at[p, 0], other),
            send(ssb.at[p, pl.ds((1 - c) * 4, 4)], pair_ss.at[p], ps.at[p, 1], pr.at[p, 1], other),
        ]
        rows = xs[p, pl.ds(c * 4, 4)].reshape(128, 1024)
        for start, width in TILES:
            block = transposed_dot(rows, gu[start : start + width, :])
            own[p, :, :, start : start + width] = block.reshape(4, 32, width)
        return pair

    def cross(p, before):
        for copy in before:
            copy.wait_recv()
        copies = []
        for k in (2, 1, 3):
            xx = past(x, k, NX)
            x_out[p, k] = (own[p, xx] + pair_in[p, xx].astype(jnp.float32)).astype(jnp.bfloat16)
            x_ss_out[p, k] = ssb[p, c * 4 + xx] + pair_ss[p, xx]
            device = at(z, y, xx, c)
            copies.append(send(x_out.at[p, k], x_in.at[p, k], xsd.at[p, 0, k], xrv.at[p, 0, k], device))
            copies.append(send(x_ss_out.at[p, k], x_ss_in.at[p, k], xsd.at[p, 1, k], xrv.at[p, 1, k], device))
        return copies

    def activate(p, before):
        total = own[p, x] + pair_in[p, x].astype(jnp.float32)
        squares = ssb[p, c * 4 + x] + pair_ss[p, x]
        for copy in before:
            copy.wait_recv()
        for k in range(1, NX):
            total = total + x_in[p, k].astype(jnp.float32)
            squares = squares + x_ss_in[p, k]
        mean_square = jnp.sum(jnp.where(diagonal, squares, 0.0), axis=1, keepdims=True) / D
        total = total * lax.rsqrt(mean_square + epsilon)
        gate = total[:, :512]
        silu = gate / (1.0 + jnp.exp(-gate))
        act[p, ffn, :, :MAIN] = (silu[:, :MAIN] * total[:, 512:]).astype(jnp.bfloat16)
        tail = silu[:, MAIN:] * pltpu.roll(total[:, MAIN:512], 64, 1)
        act[p, ffn, :, MAIN:] = tail[:, : UNITS - MAIN].astype(jnp.bfloat16)
        copies = []
        for k in (2, 1, 3):
            device = at(z, y, past(x, k, NX), c)
            copies.append(send(act.at[p, ffn], act.at[p, ffn], acs.at[p, k], acr.at[p, k], device))
        return copies, [send(act.at[p, ffn], act.at[p, ffn], fws.at[p, 0], fwr.at[p, 0], other)]

    def forward(p, before):
        copies, passed = before
        for k, copy in zip((2, 1, 3), copies):
            copy.wait_recv()
            block = past(x, NX - k, NX) * 2 + c
            passed.append(send(act.at[p, block], act.at[p, block], fws.at[p, k], fwr.at[p, k], other))
        return passed

    def lower(p, before):
        for copy in before:
            copy.wait_recv()
        rows = act[p].reshape(256, UNITS)
        copies = []
        for half, (buffer, back) in enumerate(((da, ra), (db, rb))):
            quarters = [
                jnp.dot(rows, down[:, start : start + QUARTER], preferred_element_type=jnp.float32)
                for start in (half * 512, half * 512 + QUARTER)
            ]
            low, high = exchange(*[quarter.reshape(32, 8, QUARTER) for quarter in quarters])
            blocks = jnp.stack([low, high], axis=1).astype(jnp.bfloat16).reshape(N, N, 8, QUARTER)
            if half == 0:
                buffer[p] = blocks
            else:
                for i in range(N):
                    buffer[p, :, i] = blocks[i]
            for k in range(1, N):
                there, device = along(half == 0, k)
                copies.append(
                    send(buffer.at[p, there], back.at[p, k], r1s.at[p, half, k], r1r.at[p, half, k], device)
                )
        return copies

    def reduce_second(p, before):
        copies = []
        for half, (buffer, back, onward, last) in enumerate(((da, ra, d2a, r2a), (db, rb, d2b, r2b))):
            here = z if half == 0 else y
            for copy in before[half * 7 : half * 7 + 7]:
                copy.wait_recv()
            added = buffer[p, here].astype(jnp.float32)
            for k in range(1, N):
                added = added + back[p, k].astype(jnp.float32)
            onward[p] = added.astype(jnp.bfloat16)
            for k in range(1, N):
                there, device = along(half == 1, k)
                copies.append(
                    send(onward.at[p, there], last.at[p, k], r2s.at[p, half, k], r2r.at[p, half, k], device)
                )
        return copies

    def finish(p, before):
        sums = []
        for half, (onward, last) in enumerate(((d2a, r2a), (d2b, r2b))):
            here = y if half == 0 else z
            for copy in before[half * 7 : half * 7 + 7]:
                copy.wait_recv()
            added = onward[p, here].astype(jnp.float32)
            for k in range(1, N):
                added = added + last[p, k].astype(jnp.float32)
            sums.append(added)
        return sums

    first = [gather_first(p) for p in range(PARTS)]
    second = [gather_second(p, first[p]) for p in range(PARTS)]
    across = [cross(p, multiply(p, second[p])) for p in range(PARTS)]
    spread = [forward(p, activate(p, across[p])) for p in range(PARTS)]
    reduced = [lower(p, spread[p]) for p in range(PARTS)]
    onward = [reduce_second(p, reduced[p]) for p in range(PARTS)]
    sums = [finish(p, onward[p]) for p in range(PARTS)]
    for half in range(2):
        low, high = exchange(sums[0][half], sums[1][half])
        out_ref[:, half * 512 : half * 512 + QUARTER] = low
        out_ref[:, half * 512 + QUARTER : half * 512 + 512] = high
    for copy in sent:
        copy.wait_send()


def feed_forward(hidden, gain, gate_weight, up_weight, down_weight):
    bf, f32 = jnp.bfloat16, jnp.float32
    dma = pltpu.SemaphoreType.DMA
    vmem = pltpu.VMEM
    return pl.pallas_call(
        kernel,
        out_shape=jax.ShapeDtypeStruct((8, 1024), f32),
        in_specs=[pl.BlockSpec(memory_space=vmem)] * 2 + [pl.BlockSpec(memory_space=pl.ANY)] * 3,
        out_specs=pl.BlockSpec(memory_space=vmem),
        scratch_shapes=[
            vmem((896, 1024), bf),
            vmem((UNITS, 1024), bf),
            vmem((PARTS, N, N, 8, QUARTER), bf),
            vmem((PARTS, N, N, 8, QUARTER), bf),
            vmem((PARTS, N, 32, 1024), bf),
            vmem((PARTS, N, 1, 128), f32),
            vmem((PARTS, 4, 32, 896), bf),
            vmem((PARTS, 4, 32, 896), bf),
            vmem((PARTS, 4, 1, 128), f32),
            vmem((PARTS, 4, 32, 896), f32),
            vmem((PARTS, NX, 32, 896), bf),
            vmem((PARTS, NX, 32, 896), bf),
            vmem((PARTS, NX, 1, 128), f32),
            vmem((PARTS, NX, 1, 128), f32),
            vmem((PARTS, 2 * NX, 32, UNITS), bf),
            vmem((PARTS, N, N, 8, QUARTER), bf),
            vmem((PARTS, N, N, 8, QUARTER), bf),
            vmem((PARTS, N, N, 8, QUARTER), bf),
            vmem((PARTS, N, N, 8, QUARTER), bf),
            vmem((PARTS, N, 8, QUARTER), bf),
            vmem((PARTS, N, 8, QUARTER), bf),
            vmem((PARTS, N, 8, QUARTER), bf),
            vmem((PARTS, N, 8, QUARTER), bf),
            dma((4,)),
            dma((PARTS, 2, N)),
            dma((PARTS, 2, N)),
            dma((PARTS, 2, N)),
            dma((PARTS, 2, N)),
            dma((PARTS, 2)),
            dma((PARTS, 2)),
            dma((PARTS, 2, NX)),
            dma((PARTS, 2, NX)),
            dma((PARTS, NX)),
            dma((PARTS, NX)),
            dma((PARTS, NX)),
            dma((PARTS, NX)),
            dma((PARTS, 2, N)),
            dma((PARTS, 2, N)),
            dma((PARTS, 2, N)),
            dma((PARTS, 2, N)),
        ],
        compiler_params=pltpu.CompilerParams(
            collective_id=0, has_side_effects=True, vmem_limit_bytes=40 * 1024 * 1024
        ),
        cost_estimate=pl.CostEstimate(flops=1_400_000_000, bytes_accessed=3_000_000, transcendentals=0),
        name="feed_forward",
    )(hidden, gain, gate_weight, up_weight, down_weight)


def on_device(
    residual,
    queries,
    cache_keys,
    cache_values,
    new_keys,
    new_values,
    lengths,
    counts,
    norm_gain,
    gate_weight,
    up_weight,
    down_weight,
):
    slot_count = residual.shape[0]
    width_dev = residual.shape[1]
    attention = attend(queries, cache_keys, cache_values, new_keys, new_values, lengths)
    hidden = (residual.astype(jnp.float32) + attention.astype(jnp.float32)).astype(jnp.bfloat16)
    gain_block = lax.dynamic_slice_in_dim(norm_gain, lax.axis_index("ffn") * width_dev, width_dev)
    gain = gain_block.astype(jnp.float32)[None, :]
    ffn_out = feed_forward(hidden, gain, gate_weight, up_weight, down_weight)
    is_live = jnp.arange(slot_count, dtype=jnp.int32) < counts[0]
    result = jnp.where(is_live[:, None], hidden.astype(jnp.float32) + ffn_out, 0.0)
    return result.astype(jnp.bfloat16)


def solution(mesh):
    return jax.shard_map(
        on_device,
        mesh=mesh,
        in_specs=(
            P("attn", "ffn"),
            P("attn", "ffn"),
            P("attn", "ffn", None, None),
            P("attn", "ffn", None, None),
            P("attn", "ffn", None),
            P("attn", "ffn", None),
            P("attn"),
            P("attn"),
            P(),
            P("attn", "ffn"),
            P("attn", "ffn"),
            P("attn", "ffn"),
        ),
        out_specs=P("attn", "ffn"),
        check_vma=False,
    )
```

```python
import jax
import jax.numpy as jnp
from jax import lax
from jax.experimental import pallas as pl
from jax.experimental.pallas import tpu as pltpu
from jax.sharding import PartitionSpec as P

D = 8192


epsilon = 1e-05


MESH = pl.DeviceIdType.MESH
N = 8
NX = 4
PARTS = 2
QUARTER = 256
UNITS = 448
MAIN = 384
TILES = ((0, 256), (256, 256), (512, 256), (768, 128))


def transposed_dot(rows, weight):
    return lax.dot_general(rows, weight, (((1,), (1,)), ((), ())), preferred_element_type=jnp.float32)


def exchange(low, high):
    axis = low.ndim - 2
    upper = lax.broadcasted_iota(jnp.int32, low.shape, axis) < 4
    return jnp.where(upper, low, pltpu.roll(high, 4, axis)), jnp.where(upper, pltpu.roll(low, 4, axis), high)


def attend(
    inputs,
    queries_ref,
    keys_ref,
    values_ref,
    new_keys_ref,
    new_values_ref,
    lengths_ref,
    residual_ref,
    by_head,
    hidden_ref,
):
    for load in inputs[:4]:
        load.wait()
    score_scale = 1.0 / 128**0.5
    for h in range(8):
        by_head[h * 8 : h * 8 + 8, :] = queries_ref[:, h * 128 : h * 128 + 128].astype(jnp.float32)
    new_keys = new_keys_ref[...].astype(jnp.float32)
    position = lax.broadcasted_iota(jnp.int32, (8, 512), 1)
    scores = []
    own = []
    for r in range(8):
        query = by_head[pl.ds(r, 8, stride=8), :]
        own.append(jnp.sum(query * new_keys[r : r + 1, :], axis=1, keepdims=True))
        slot = transposed_dot(query.astype(jnp.bfloat16), keys_ref[r]) * score_scale
        scores.append(jnp.where(position < lengths_ref[r], slot, -1e30))
    scores = jnp.concatenate(scores, axis=0)
    own = jnp.concatenate(own, axis=0) * score_scale
    row_max = jnp.maximum(jnp.max(scores, axis=1, keepdims=True), own)
    key_weights = jnp.exp(scores - row_max)
    own_weight = jnp.exp(own - row_max)
    denominator = jnp.sum(key_weights, axis=1, keepdims=True) + own_weight
    key_probs = key_weights / denominator
    own_prob = (own_weight / denominator).astype(jnp.bfloat16).astype(jnp.float32)
    for load in inputs[4:]:
        load.wait()
    new_values = new_values_ref[...].astype(jnp.float32)
    for r in range(8):
        probs = key_probs[r * 8 : r * 8 + 8, :].astype(jnp.bfloat16)
        mixed = jnp.dot(probs, values_ref[r], preferred_element_type=jnp.float32)
        mixed = mixed + own_prob[r * 8 : r * 8 + 8, :] * new_values[r : r + 1, :]
        by_head[pl.ds(r, 8, stride=8), :] = mixed.astype(jnp.bfloat16).astype(jnp.float32)
    for h in range(8):
        lanes = slice(h * 128, h * 128 + 128)
        hidden = residual_ref[:, lanes].astype(jnp.float32) + by_head[h * 8 : h * 8 + 8, :]
        hidden_ref[:, lanes] = hidden.astype(jnp.bfloat16).astype(jnp.float32)


def kernel(
    residual_hbm,
    queries_hbm,
    keys_hbm,
    values_hbm,
    new_keys_hbm,
    new_values_hbm,
    lengths_hbm,
    counts_hbm,
    gain_hbm,
    gate_hbm,
    up_hbm,
    down_hbm,
    out_ref,
    residual_ref,
    queries_ref,
    keys_ref,
    values_ref,
    new_keys_ref,
    new_values_ref,
    lengths_ref,
    counts_ref,
    gain_ref,
    by_head,
    hidden_ref,
    gu,
    down,
    ga,
    gb,
    xs,
    ssb,
    pair_out,
    pair_in,
    pair_ss,
    own,
    x_out,
    x_in,
    x_ss_out,
    x_ss_in,
    act,
    da,
    db,
    ra,
    rb,
    d2a,
    d2b,
    r2a,
    r2b,
    asem,
    wsem,
    g1s,
    g1r,
    g2s,
    g2r,
    ps,
    pr,
    xsd,
    xrv,
    acs,
    acr,
    fws,
    fwr,
    r1s,
    r1r,
    r2s,
    r2r,
):
    attn = lax.axis_index("attn")
    ffn = lax.axis_index("ffn")
    z, y = lax.div(attn, N), lax.rem(attn, N)
    x, c = lax.div(ffn, 2), lax.rem(ffn, 2)

    def at(zz, yy, xx, cc):
        return (zz * N + yy, xx * 2 + cc)

    def past(i, k, n):
        return lax.rem(i + k, n)

    inputs = [
        pltpu.make_async_copy(source, target, asem.at[i])
        for i, (source, target) in enumerate(
            (
                (queries_hbm, queries_ref),
                (new_keys_hbm, new_keys_ref),
                (lengths_hbm, lengths_ref),
                (keys_hbm, keys_ref),
                (values_hbm, values_ref),
                (new_values_hbm, new_values_ref),
                (residual_hbm, residual_ref),
                (counts_hbm, counts_ref),
                (gain_hbm.at[pl.ds(ffn * 1024, 1024)], gain_ref),
            )
        )
    ]
    for load in inputs:
        load.start()
    loads = [
        pltpu.make_async_copy(gate_hbm, gu.at[pl.ds(0, UNITS)], wsem.at[0]),
        pltpu.make_async_copy(up_hbm.at[pl.ds(MAIN, UNITS - MAIN)], gu.at[pl.ds(UNITS, UNITS - MAIN)], wsem.at[1]),
        pltpu.make_async_copy(up_hbm.at[pl.ds(0, MAIN)], gu.at[pl.ds(512, MAIN)], wsem.at[2]),
        pltpu.make_async_copy(down_hbm, down, wsem.at[3]),
    ]
    for load in loads:
        load.start()

    barrier = pltpu.get_barrier_semaphore()
    partners = [at(past(z, k, N), y, x, c) for k in range(1, N)]
    partners += [at(z, past(y, k, N), x, c) for k in range(1, N)]
    partners += [at(z, y, past(x, k, NX), c) for k in range(1, NX)]
    partners += [at(z, y, x, 1 - c)]
    for partner in partners:
        pl.semaphore_signal(barrier, inc=1, device_id=partner, device_id_type=MESH)

    attend(
        inputs,
        queries_ref,
        keys_ref,
        values_ref,
        new_keys_ref,
        new_values_ref,
        lengths_ref,
        residual_ref,
        by_head,
        hidden_ref,
    )
    gain = gain_ref[...].astype(jnp.float32).reshape(1, 1024)
    pl.semaphore_wait(barrier, len(partners))

    sent = []

    def send(source, target, send_sem, recv_sem, device):
        copy = pltpu.make_async_remote_copy(
            src_ref=source, dst_ref=target, send_sem=send_sem, recv_sem=recv_sem, device_id=device, device_id_type=MESH
        )
        copy.start()
        sent.append(copy)
        return copy

    other = at(z, y, x, 1 - c)
    lane = lax.broadcasted_iota(jnp.int32, (32, 128), 1)
    row = lax.broadcasted_iota(jnp.int32, (32, 128), 0)
    diagonal = lane == row

    def along(first_is_z, k):
        if first_is_z:
            return past(z, k, N), at(past(z, k, N), y, x, c)
        return past(y, k, N), at(z, past(y, k, N), x, c)

    wide = hidden_ref[...]
    for buffer, start, one, two in ((ga, 0, z, y), (gb, 512, y, z)):
        blocks = exchange(wide[:, start : start + QUARTER], wide[:, start + QUARTER : start + 512])
        for p in range(PARTS):
            buffer[p, one, two] = blocks[p].astype(jnp.bfloat16)

    def gather_first(p):
        copies = []
        for k in range(1, N):
            copies.append(send(ga.at[p, z, y], ga.at[p, z, y], g1s.at[p, 0, k], g1r.at[p, 0, k], along(False, k)[1]))
            copies.append(send(gb.at[p, y, z], gb.at[p, y, z], g1s.at[p, 1, k], g1r.at[p, 1, k], along(True, k)[1]))
        return copies

    def gather_second(p, before):
        for copy in before:
            copy.wait_recv()
        copies = []
        for k in range(1, N):
            copies.append(send(ga.at[p, z], ga.at[p, z], g2s.at[p, 0, k], g2r.at[p, 0, k], along(True, k)[1]))
            copies.append(send(gb.at[p, y], gb.at[p, y], g2s.at[p, 1, k], g2r.at[p, 1, k], along(False, k)[1]))
        return copies

    def rows_of(packed):
        packed = packed.astype(jnp.float32).reshape(4, 2, 8, QUARTER)
        low, high = exchange(packed[:, 0], packed[:, 1])
        return [low.reshape(32, QUARTER), high.reshape(32, QUARTER)]

    def multiply(p, before):
        for copy in before:
            copy.wait_recv()

        def scale(zz, carry):
            place = lax.rem(zz, 2) * 4 + lax.div(zz, 2)
            quarters = rows_of(ga[p, zz]) + rows_of(gb[p, :, zz])
            squares = quarters[0] * quarters[0]
            for part in quarters[1:]:
                squares = squares + part * part
            squares = jnp.sum(squares, axis=1, keepdims=True)
            ssb[p, place] = jnp.sum(jnp.where(diagonal, squares, 0.0), axis=0, keepdims=True)
            for i, part in enumerate(quarters):
                lanes = slice(i * QUARTER, (i + 1) * QUARTER)
                xs[p, place, :, lanes] = (part * gain[:, lanes]).astype(jnp.bfloat16)
            return carry

        lax.fori_loop(0, N, scale, 0)
        if p == 0:
            for load in loads:
                load.wait()
        rows = xs[p, pl.ds((1 - c) * 4, 4)].reshape(128, 1024)
        for start, width in TILES:
            block = transposed_dot(rows, gu[start : start + width, :])
            pair_out[p, :, :, start : start + width] = block.astype(jnp.bfloat16).reshape(4, 32, width)
        pair = [
            send(pair_out.at[p], pair_in.at[p], ps.at[p, 0], pr.at[p, 0], other),
            send(ssb.at[p, pl.ds((1 - c) * 4, 4)], pair_ss.at[p], ps.at[p, 1], pr.at[p, 1], other),
        ]
        rows = xs[p, pl.ds(c * 4, 4)].reshape(128, 1024)
        for start, width in TILES:
            block = transposed_dot(rows, gu[start : start + width, :])
            own[p, :, :, start : start + width] = block.reshape(4, 32, width)
        return pair

    def cross(p, before):
        for copy in before:
            copy.wait_recv()
        copies = []
        for k in (2, 1, 3):
            xx = past(x, k, NX)
            x_out[p, k] = (own[p, xx] + pair_in[p, xx].astype(jnp.float32)).astype(jnp.bfloat16)
            x_ss_out[p, k] = ssb[p, c * 4 + xx] + pair_ss[p, xx]
            device = at(z, y, xx, c)
            copies.append(send(x_out.at[p, k], x_in.at[p, k], xsd.at[p, 0, k], xrv.at[p, 0, k], device))
            copies.append(send(x_ss_out.at[p, k], x_ss_in.at[p, k], xsd.at[p, 1, k], xrv.at[p, 1, k], device))
        return copies

    def activate(p, before):
        total = own[p, x] + pair_in[p, x].astype(jnp.float32)
        squares = ssb[p, c * 4 + x] + pair_ss[p, x]
        for copy in before:
            copy.wait_recv()
        for k in range(1, NX):
            total = total + x_in[p, k].astype(jnp.float32)
            squares = squares + x_ss_in[p, k]
        mean_square = jnp.sum(jnp.where(diagonal, squares, 0.0), axis=1, keepdims=True) / D
        total = total * lax.rsqrt(mean_square + epsilon)
        gate = total[:, :512]
        silu = gate / (1.0 + jnp.exp(-gate))
        act[p, ffn, :, :MAIN] = (silu[:, :MAIN] * total[:, 512:]).astype(jnp.bfloat16)
        tail = silu[:, MAIN:] * pltpu.roll(total[:, MAIN:512], 64, 1)
        act[p, ffn, :, MAIN:] = tail[:, : UNITS - MAIN].astype(jnp.bfloat16)
        copies = []
        for k in (2, 1, 3):
            device = at(z, y, past(x, k, NX), c)
            copies.append(send(act.at[p, ffn], act.at[p, ffn], acs.at[p, k], acr.at[p, k], device))
        return copies, [send(act.at[p, ffn], act.at[p, ffn], fws.at[p, 0], fwr.at[p, 0], other)]

    def forward(p, before):
        copies, passed = before
        for k, copy in zip((2, 1, 3), copies):
            copy.wait_recv()
            block = past(x, NX - k, NX) * 2 + c
            passed.append(send(act.at[p, block], act.at[p, block], fws.at[p, k], fwr.at[p, k], other))
        return passed

    def lower(p, before):
        for copy in before:
            copy.wait_recv()
        rows = act[p].reshape(256, UNITS)
        copies = []
        for half, (buffer, back) in enumerate(((da, ra), (db, rb))):
            quarters = [
                jnp.dot(rows, down[:, start : start + QUARTER], preferred_element_type=jnp.float32)
                for start in (half * 512, half * 512 + QUARTER)
            ]
            low, high = exchange(*[quarter.reshape(32, 8, QUARTER) for quarter in quarters])
            blocks = jnp.stack([low, high], axis=1).astype(jnp.bfloat16).reshape(N, N, 8, QUARTER)
            if half == 0:
                buffer[p] = blocks
            else:
                for i in range(N):
                    buffer[p, :, i] = blocks[i]
            for k in range(1, N):
                there, device = along(half == 0, k)
                copies.append(
                    send(buffer.at[p, there], back.at[p, k], r1s.at[p, half, k], r1r.at[p, half, k], device)
                )
        return copies

    def reduce_second(p, before):
        copies = []
        for half, (buffer, back, onward, last) in enumerate(((da, ra, d2a, r2a), (db, rb, d2b, r2b))):
            here = z if half == 0 else y
            for copy in before[half * 7 : half * 7 + 7]:
                copy.wait_recv()
            added = buffer[p, here].astype(jnp.float32)
            for k in range(1, N):
                added = added + back[p, k].astype(jnp.float32)
            onward[p] = added.astype(jnp.bfloat16)
            for k in range(1, N):
                there, device = along(half == 1, k)
                copies.append(
                    send(onward.at[p, there], last.at[p, k], r2s.at[p, half, k], r2r.at[p, half, k], device)
                )
        return copies

    def finish(p, before):
        sums = []
        for half, (onward, last) in enumerate(((d2a, r2a), (d2b, r2b))):
            here = y if half == 0 else z
            for copy in before[half * 7 : half * 7 + 7]:
                copy.wait_recv()
            added = onward[p, here].astype(jnp.float32)
            for k in range(1, N):
                added = added + last[p, k].astype(jnp.float32)
            sums.append(added)
        return sums

    first = [gather_first(p) for p in range(PARTS)]
    second = [gather_second(p, first[p]) for p in range(PARTS)]
    across = [cross(p, multiply(p, second[p])) for p in range(PARTS)]
    spread = [forward(p, activate(p, across[p])) for p in range(PARTS)]
    reduced = [lower(p, spread[p]) for p in range(PARTS)]
    onward = [reduce_second(p, reduced[p]) for p in range(PARTS)]
    sums = [finish(p, onward[p]) for p in range(PARTS)]
    live = lax.broadcasted_iota(jnp.int32, (8, QUARTER), 0) < counts_ref[0]
    for half in range(2):
        for i, part in enumerate(exchange(sums[0][half], sums[1][half])):
            lanes = slice(half * 512 + i * QUARTER, half * 512 + (i + 1) * QUARTER)
            out_ref[:, lanes] = jnp.where(live, hidden_ref[:, lanes] + part, 0.0).astype(jnp.bfloat16)
    for copy in sent:
        copy.wait_send()


def whole_layer(*operands):
    bf, f32 = jnp.bfloat16, jnp.float32
    dma = pltpu.SemaphoreType.DMA
    vmem = pltpu.VMEM
    return pl.pallas_call(
        kernel,
        out_shape=jax.ShapeDtypeStruct((8, 1024), bf),
        in_specs=[pl.BlockSpec(memory_space=pltpu.HBM)] * 12,
        out_specs=pl.BlockSpec(memory_space=vmem),
        scratch_shapes=[
            vmem((8, 1024), bf),
            vmem((8, 1024), bf),
            vmem((8, 512, 128), bf),
            vmem((8, 512, 128), bf),
            vmem((8, 128), bf),
            vmem((8, 128), bf),
            pltpu.SMEM((8,), jnp.int32),
            pltpu.SMEM((1,), jnp.int32),
            vmem((1024,), bf),
            vmem((64, 128), f32),
            vmem((8, 1024), f32),
            vmem((896, 1024), bf),
            vmem((UNITS, 1024), bf),
            vmem((PARTS, N, N, 8, QUARTER), bf),
            vmem((PARTS, N, N, 8, QUARTER), bf),
            vmem((PARTS, N, 32, 1024), bf),
            vmem((PARTS, N, 1, 128), f32),
            vmem((PARTS, 4, 32, 896), bf),
            vmem((PARTS, 4, 32, 896), bf),
            vmem((PARTS, 4, 1, 128), f32),
            vmem((PARTS, 4, 32, 896), f32),
            vmem((PARTS, NX, 32, 896), bf),
            vmem((PARTS, NX, 32, 896), bf),
            vmem((PARTS, NX, 1, 128), f32),
            vmem((PARTS, NX, 1, 128), f32),
            vmem((PARTS, 2 * NX, 32, UNITS), bf),
            vmem((PARTS, N, N, 8, QUARTER), bf),
            vmem((PARTS, N, N, 8, QUARTER), bf),
            vmem((PARTS, N, N, 8, QUARTER), bf),
            vmem((PARTS, N, N, 8, QUARTER), bf),
            vmem((PARTS, N, 8, QUARTER), bf),
            vmem((PARTS, N, 8, QUARTER), bf),
            vmem((PARTS, N, 8, QUARTER), bf),
            vmem((PARTS, N, 8, QUARTER), bf),
            dma((9,)),
            dma((4,)),
            dma((PARTS, 2, N)),
            dma((PARTS, 2, N)),
            dma((PARTS, 2, N)),
            dma((PARTS, 2, N)),
            dma((PARTS, 2)),
            dma((PARTS, 2)),
            dma((PARTS, 2, NX)),
            dma((PARTS, 2, NX)),
            dma((PARTS, NX)),
            dma((PARTS, NX)),
            dma((PARTS, NX)),
            dma((PARTS, NX)),
            dma((PARTS, 2, N)),
            dma((PARTS, 2, N)),
            dma((PARTS, 2, N)),
            dma((PARTS, 2, N)),
        ],
        compiler_params=pltpu.CompilerParams(
            collective_id=0, has_side_effects=True, vmem_limit_bytes=60 * 1024 * 1024
        ),
        cost_estimate=pl.CostEstimate(flops=1_430_000_000, bytes_accessed=5_000_000, transcendentals=0),
        name="whole_layer",
    )(*operands)


def on_device(
    residual,
    queries,
    cache_keys,
    cache_values,
    new_keys,
    new_values,
    lengths,
    counts,
    norm_gain,
    gate_weight,
    up_weight,
    down_weight,
):
    return whole_layer(
        residual,
        queries,
        cache_keys.reshape(8, 512, 128),
        cache_values.reshape(8, 512, 128),
        new_keys.reshape(8, 128),
        new_values.reshape(8, 128),
        lengths,
        counts,
        norm_gain,
        gate_weight,
        up_weight,
        down_weight,
    )


def solution(mesh):
    return jax.shard_map(
        on_device,
        mesh=mesh,
        in_specs=(
            P("attn", "ffn"),
            P("attn", "ffn"),
            P("attn", "ffn", None, None),
            P("attn", "ffn", None, None),
            P("attn", "ffn", None),
            P("attn", "ffn", None),
            P("attn"),
            P("attn"),
            P(),
            P("attn", "ffn"),
            P("attn", "ffn"),
            P("attn", "ffn"),
        ),
        out_specs=P("attn", "ffn"),
        check_vma=False,
    )
```

```python
import jax
import jax.numpy as jnp
from jax import lax
from jax.experimental import pallas as pl
from jax.experimental.pallas import tpu as pltpu
from jax.sharding import PartitionSpec as P

D = 8192


epsilon = 1e-05


MESH = pl.DeviceIdType.MESH
N = 8
NX = 4
HALF = 512
UNITS = 448
MAIN = 384
TILES = ((0, 256), (256, 256), (512, 256), (768, 128))
STEPS = (0, 1, -1, 2, -2, 3, -3, 4)
GROUPS = ((0, 1, 2, 3, 4), (5, 6, 7))


def transposed_dot(rows, weight):
    return lax.dot_general(rows, weight, (((1,), (1,)), ((), ())), preferred_element_type=jnp.float32)


def exchange(low, high):
    axis = low.ndim - 2
    upper = lax.broadcasted_iota(jnp.int32, low.shape, axis) < 4
    return jnp.where(upper, low, pltpu.roll(high, 4, axis)), jnp.where(upper, pltpu.roll(low, 4, axis), high)


def attend(
    inputs,
    queries_ref,
    keys_ref,
    values_ref,
    new_keys_ref,
    new_values_ref,
    lengths_ref,
    residual_ref,
    by_head,
    hidden_ref,
):
    for load in inputs[:4]:
        load.wait()
    score_scale = 1.0 / 128**0.5
    for h in range(8):
        by_head[h * 8 : h * 8 + 8, :] = queries_ref[:, h * 128 : h * 128 + 128].astype(jnp.float32)
    new_keys = new_keys_ref[...].astype(jnp.float32)
    position = lax.broadcasted_iota(jnp.int32, (8, 512), 1)
    scores = []
    own = []
    for r in range(8):
        query = by_head[pl.ds(r, 8, stride=8), :]
        own.append(jnp.sum(query * new_keys[r : r + 1, :], axis=1, keepdims=True))
        slot = transposed_dot(query.astype(jnp.bfloat16), keys_ref[r]) * score_scale
        scores.append(jnp.where(position < lengths_ref[r], slot, -1e30))
    scores = jnp.concatenate(scores, axis=0)
    own = jnp.concatenate(own, axis=0) * score_scale
    row_max = jnp.maximum(jnp.max(scores, axis=1, keepdims=True), own)
    key_weights = jnp.exp(scores - row_max)
    own_weight = jnp.exp(own - row_max)
    denominator = jnp.sum(key_weights, axis=1, keepdims=True) + own_weight
    key_probs = key_weights / denominator
    own_prob = (own_weight / denominator).astype(jnp.bfloat16).astype(jnp.float32)
    for load in inputs[4:]:
        load.wait()
    new_values = new_values_ref[...].astype(jnp.float32)
    for r in range(8):
        probs = key_probs[r * 8 : r * 8 + 8, :].astype(jnp.bfloat16)
        mixed = jnp.dot(probs, values_ref[r], preferred_element_type=jnp.float32)
        mixed = mixed + own_prob[r * 8 : r * 8 + 8, :] * new_values[r : r + 1, :]
        by_head[pl.ds(r, 8, stride=8), :] = mixed.astype(jnp.bfloat16).astype(jnp.float32)
    for h in range(8):
        lanes = slice(h * 128, h * 128 + 128)
        hidden = residual_ref[:, lanes].astype(jnp.float32) + by_head[h * 8 : h * 8 + 8, :]
        hidden_ref[:, lanes] = hidden.astype(jnp.bfloat16).astype(jnp.float32)


def kernel(
    residual_hbm,
    queries_hbm,
    keys_hbm,
    values_hbm,
    new_keys_hbm,
    new_values_hbm,
    lengths_hbm,
    counts_hbm,
    gain_hbm,
    gate_hbm,
    up_hbm,
    down_hbm,
    out_ref,
    residual_ref,
    queries_ref,
    keys_ref,
    values_ref,
    new_keys_ref,
    new_values_ref,
    lengths_ref,
    counts_ref,
    gain_ref,
    by_head,
    hidden_ref,
    gu,
    down,
    held,
    terms,
    back,
    onward,
    last,
    asem,
    wsem,
    g1s,
    g1r,
    g2s,
    g2r,
    r1s,
    r1r,
    r2s,
    r2r,
    *by_group,
):
    each = len(by_group) // len(GROUPS)
    by_group = [by_group[g * each : g * each + each] for g in range(len(GROUPS))]
    attn = lax.axis_index("attn")
    ffn = lax.axis_index("ffn")
    z, y = lax.div(attn, N), lax.rem(attn, N)
    x, c = lax.div(ffn, 2), lax.rem(ffn, 2)

    def at(zz, yy, xx, cc):
        return (zz * N + yy, xx * 2 + cc)

    def past(i, k, n):
        return lax.rem(i + k, n)

    inputs = [
        pltpu.make_async_copy(source, target, asem.at[i])
        for i, (source, target) in enumerate(
            (
                (queries_hbm, queries_ref),
                (new_keys_hbm, new_keys_ref),
                (lengths_hbm, lengths_ref),
                (keys_hbm, keys_ref),
                (values_hbm, values_ref),
                (new_values_hbm, new_values_ref),
                (residual_hbm, residual_ref),
                (counts_hbm, counts_ref),
                (gain_hbm.at[pl.ds(ffn * 1024, 1024)], gain_ref),
            )
        )
    ]
    for load in inputs:
        load.start()
    loads = [
        pltpu.make_async_copy(gate_hbm, gu.at[pl.ds(0, UNITS)], wsem.at[0]),
        pltpu.make_async_copy(up_hbm.at[pl.ds(MAIN, UNITS - MAIN)], gu.at[pl.ds(UNITS, UNITS - MAIN)], wsem.at[1]),
        pltpu.make_async_copy(up_hbm.at[pl.ds(0, MAIN)], gu.at[pl.ds(512, MAIN)], wsem.at[2]),
        pltpu.make_async_copy(down_hbm, down, wsem.at[3]),
    ]
    for load in loads:
        load.start()

    barrier = pltpu.get_barrier_semaphore()
    partners = [at(past(z, k, N), y, x, c) for k in range(1, N)]
    partners += [at(z, past(y, k, N), x, c) for k in range(1, N)]
    partners += [at(z, y, past(x, k, NX), c) for k in range(1, NX)]
    partners += [at(z, y, x, 1 - c)]
    for partner in partners:
        pl.semaphore_signal(barrier, inc=1, device_id=partner, device_id_type=MESH)

    attend(
        inputs,
        queries_ref,
        keys_ref,
        values_ref,
        new_keys_ref,
        new_values_ref,
        lengths_ref,
        residual_ref,
        by_head,
        hidden_ref,
    )
    gain = gain_ref[...].astype(jnp.float32).reshape(1, 1024)
    pl.semaphore_wait(barrier, len(partners))

    sent = []

    def send(source, target, send_sem, recv_sem, device):
        copy = pltpu.make_async_remote_copy(
            src_ref=source, dst_ref=target, send_sem=send_sem, recv_sem=recv_sem, device_id=device, device_id_type=MESH
        )
        copy.start()
        sent.append(copy)
        return copy

    other = at(z, y, x, 1 - c)

    def along(is_z, step):
        if is_z:
            return at(lax.rem(z + (N + step), N), y, x, c)
        return at(z, lax.rem(y + (N + step), N), x, c)

    blocks = exchange(hidden_ref[:, :HALF], hidden_ref[:, HALF:])
    first, second = [[], []], [{}, {}]
    for route in range(2):
        held[route, 0, 0] = blocks[route].astype(jnp.bfloat16)
    for i in (7, 5, 6, 3, 4, 1, 2):
        for route in range(2):
            first[route].append(
                send(
                    held.at[route, 0, 0],
                    held.at[route, 0, i],
                    g1s.at[route, i],
                    g1r.at[route, i],
                    along(route == 1, -STEPS[i]),
                )
            )

    def pass_on(route, i, source, device):
        second[route][i] = send(
            held.at[route, source], held.at[route, i], g2s.at[route, i], g2r.at[route, i], device
        )

    for route in range(2):
        for copy in first[route]:
            copy.wait_recv()
        for i in (3, 4, 1, 2):
            pass_on(route, i, 0, along(route == 0, -STEPS[i]))
    for route in range(2):
        second[route][3].wait_recv()
        second[route][4].wait_recv()
        pass_on(route, 7, 3 + c, along(route == 0, -2 + 4 * c))
        pass_on(route, 5, 3, along(route == 0, -1))
        pass_on(route, 6, 4, along(route == 0, 1))

    def multiply(g):
        xs, ssb, pair_out, pair_in, pair_ss, own = by_group[g][:6]
        places = GROUPS[g]
        count = len(places)
        lane = lax.broadcasted_iota(jnp.int32, (4, 8, 128), 2)
        row = lax.broadcasted_iota(jnp.int32, (4, 8, 128), 1)
        for route in range(2):
            squares = jnp.zeros((4, 1, 128), jnp.float32)
            for d, i in enumerate(places):
                if i in (1, 2, 5, 6, 7):
                    second[route][i].wait_recv()
                packed = held[route, i].astype(jnp.float32).reshape(4, 2, 8, HALF)
                low, high = exchange(packed[:, 0], packed[:, 1])
                square = jnp.sum(low * low + high * high, axis=2, keepdims=True)
                squares = squares + jnp.sum(jnp.where(lane == row + 8 * d, square, 0.0), axis=1, keepdims=True)
                xs[route * 4 : route * 4 + 4, d, :, :HALF] = (low * gain[:, :HALF]).astype(jnp.bfloat16)
                xs[route * 4 : route * 4 + 4, d, :, HALF:] = (high * gain[:, HALF:]).astype(jnp.bfloat16)
            ssb[route * 4 : route * 4 + 4] = squares
        if g == 0:
            for load in loads:
                load.wait()
        rows = xs[pl.ds((1 - c) * 4, 4)].reshape(32 * count, 1024)
        for start, width in TILES:
            block = transposed_dot(rows, gu[start : start + width, :]).astype(jnp.bfloat16)
            pair_out[:, :, :, start : start + width] = block.reshape(4, count, 8, width)
        pair = [
            send(pair_out, pair_in, by_group[g][11].at[0], by_group[g][12].at[0], other),
            send(ssb.at[pl.ds((1 - c) * 4, 4)], pair_ss, by_group[g][11].at[1], by_group[g][12].at[1], other),
        ]
        rows = xs[pl.ds(c * 4, 4)].reshape(32 * count, 1024)
        for start, width in TILES:
            block = transposed_dot(rows, gu[start : start + width, :])
            own[:, :, :, start : start + width] = block.reshape(4, count, 8, width)
        return pair

    def cross(g, before):
        ssb, _, pair_in, pair_ss, own, x_out, x_in, x_ss_out, x_ss_in = by_group[g][1:10]
        xss, xsr = by_group[g][13:15]
        for copy in before:
            copy.wait_recv()
        copies = []
        for k in (2, 1, 3):
            xx = past(x, k, NX)
            x_out[k] = (own[xx] + pair_in[xx].astype(jnp.float32)).astype(jnp.bfloat16)
            x_ss_out[k] = ssb[c * 4 + xx] + pair_ss[xx]
            device = at(z, y, xx, c)
            copies.append(send(x_out.at[k], x_in.at[k], xss.at[0, k], xsr.at[0, k], device))
            copies.append(send(x_ss_out.at[k], x_ss_in.at[k], xss.at[1, k], xsr.at[1, k], device))
        return copies

    def activate(g, before):
        ssb, _, pair_in, pair_ss, own, _, x_in, _, x_ss_in, act = by_group[g][1:11]
        acs, acr, fws, fwr = by_group[g][15:19]
        count = len(GROUPS[g])
        total = own[x] + pair_in[x].astype(jnp.float32)
        squares = ssb[c * 4 + x] + pair_ss[x]
        for copy in before:
            copy.wait_recv()
        for k in range(1, NX):
            total = total + x_in[k].astype(jnp.float32)
            squares = squares + x_ss_in[k]
        total = total.reshape(8 * count, 896)
        lane = lax.broadcasted_iota(jnp.int32, (8 * count, 128), 1)
        row = lax.broadcasted_iota(jnp.int32, (8 * count, 128), 0)
        mean_square = jnp.sum(jnp.where(lane == row, squares, 0.0), axis=1, keepdims=True) / D
        total = total * lax.rsqrt(mean_square + epsilon)
        gate = total[:, :512]
        silu = gate / (1.0 + jnp.exp(-gate))
        mine = c * 4 + x
        main = (silu[:, :MAIN] * total[:, 512:]).astype(jnp.bfloat16)
        act[mine, :, :, :MAIN] = main.reshape(count, 8, MAIN)
        tail = (silu[:, MAIN:] * pltpu.roll(total[:, MAIN:512], 64, 1))[:, : UNITS - MAIN]
        act[mine, :, :, MAIN:] = tail.astype(jnp.bfloat16).reshape(count, 8, UNITS - MAIN)
        copies = []
        for k in (2, 1, 3):
            device = at(z, y, past(x, k, NX), c)
            copies.append(send(act.at[mine], act.at[mine], acs.at[k], acr.at[k], device))
        return copies, [send(act.at[mine], act.at[mine], fws.at[0], fwr.at[0], other)]

    def forward(g, before):
        act = by_group[g][10]
        fws, fwr = by_group[g][17:19]
        copies, passed = before
        for k, copy in zip((1, 3, 2), (copies[1], copies[2], copies[0])):
            copy.wait_recv()
            place = c * 4 + past(x, NX - k, NX)
            passed.append(send(act.at[place], act.at[place], fws.at[k], fwr.at[k], other))
        return passed

    reduced = [{}, {}]

    def lower(g, before):
        act = by_group[g][10]
        places = GROUPS[g]
        count = len(places)
        for copy in before:
            copy.wait_recv()
        rows = act[...].reshape(64 * count, UNITS)
        for start in (0, 256):
            quarters = [
                jnp.dot(rows, down[:, at_lane : at_lane + 256], preferred_element_type=jnp.float32)
                for at_lane in (start, start + HALF)
            ]
            halves = exchange(*[quarter.reshape(2, 4, count, 8, 256) for quarter in quarters])
            for route in range(2):
                for d, i in enumerate(places):
                    block = jnp.stack([half[route, :, d] for half in halves], axis=1)
                    terms[route, i, :, :, start : start + 256] = block.reshape(N, 8, 256).astype(jnp.bfloat16)
        for i in reversed(places):
            for route in range(2):
                if i:
                    reduced[route][i] = send(
                        terms.at[route, i],
                        back.at[route, i],
                        r1s.at[route, i],
                        r1r.at[route, i],
                        along(route == 0, STEPS[i]),
                    )

    pairs = multiply(0)
    across = [cross(0, pairs)]
    pairs = multiply(1)
    across.append(cross(1, pairs))
    spread = [activate(g, across[g]) for g in range(2)]
    lower(0, forward(0, spread[0]))
    lower(1, forward(1, spread[1]))

    final = [[], []]
    for route in range(2):
        added = terms[route, 0].astype(jnp.float32)
        for i in range(1, N):
            reduced[route][i].wait_recv()
            added = added + back[route, i].astype(jnp.float32)
        onward[route] = added.astype(jnp.bfloat16)
        for i in (7, 5, 6, 3, 4, 1, 2):
            final[route].append(
                send(
                    onward.at[route, i],
                    last.at[route, i],
                    r2s.at[route, i],
                    r2r.at[route, i],
                    along(route == 1, STEPS[i]),
                )
            )
    sums = []
    for route in range(2):
        for copy in final[route]:
            copy.wait_recv()
        added = onward[route, 0].astype(jnp.float32)
        for i in range(1, N):
            added = added + last[route, i].astype(jnp.float32)
        sums.append(added)
    live = lax.broadcasted_iota(jnp.int32, (8, HALF), 0) < counts_ref[0]
    for half, part in enumerate(exchange(*sums)):
        lanes = slice(half * HALF, (half + 1) * HALF)
        out_ref[:, lanes] = jnp.where(live, hidden_ref[:, lanes] + part, 0.0).astype(jnp.bfloat16)
    for copy in sent:
        copy.wait_send()


def whole_layer(*operands):
    bf, f32 = jnp.bfloat16, jnp.float32
    dma = pltpu.SemaphoreType.DMA
    vmem = pltpu.VMEM
    return pl.pallas_call(
        kernel,
        out_shape=jax.ShapeDtypeStruct((8, 1024), bf),
        in_specs=[pl.BlockSpec(memory_space=pltpu.HBM)] * 12,
        out_specs=pl.BlockSpec(memory_space=vmem),
        scratch_shapes=[
            vmem((8, 1024), bf),
            vmem((8, 1024), bf),
            vmem((8, 512, 128), bf),
            vmem((8, 512, 128), bf),
            vmem((8, 128), bf),
            vmem((8, 128), bf),
            pltpu.SMEM((8,), jnp.int32),
            pltpu.SMEM((1,), jnp.int32),
            vmem((1024,), bf),
            vmem((64, 128), f32),
            vmem((8, 1024), f32),
            vmem((896, 1024), bf),
            vmem((UNITS, 1024), bf),
            vmem((2, N, N, 8, HALF), bf),
            vmem((2, N, N, 8, HALF), bf),
            vmem((2, N, N, 8, HALF), bf),
            vmem((2, N, 8, HALF), bf),
            vmem((2, N, 8, HALF), bf),
            dma((9,)),
            dma((4,)),
        ]
        + [dma((2, N))] * 8
        + [
            shape
            for count in [len(places) for places in GROUPS]
            for shape in (
                vmem((N, count, 8, 1024), bf),
                vmem((N, 1, 128), f32),
                vmem((4, count, 8, 896), bf),
                vmem((4, count, 8, 896), bf),
                vmem((4, 1, 128), f32),
                vmem((4, count, 8, 896), f32),
                vmem((NX, count, 8, 896), bf),
                vmem((NX, count, 8, 896), bf),
                vmem((NX, 1, 128), f32),
                vmem((NX, 1, 128), f32),
                vmem((2 * NX, count, 8, UNITS), bf),
                dma((2,)),
                dma((2,)),
                dma((2, NX)),
                dma((2, NX)),
                dma((NX,)),
                dma((NX,)),
                dma((NX,)),
                dma((NX,)),
            )
        ],
        compiler_params=pltpu.CompilerParams(
            collective_id=0, has_side_effects=True, vmem_limit_bytes=60 * 1024 * 1024
        ),
        cost_estimate=pl.CostEstimate(flops=1_430_000_000, bytes_accessed=5_000_000, transcendentals=0),
        name="whole_layer",
    )(*operands)


def on_device(
    residual,
    queries,
    cache_keys,
    cache_values,
    new_keys,
    new_values,
    lengths,
    counts,
    norm_gain,
    gate_weight,
    up_weight,
    down_weight,
):
    return whole_layer(
        residual,
        queries,
        cache_keys.reshape(8, 512, 128),
        cache_values.reshape(8, 512, 128),
        new_keys.reshape(8, 128),
        new_values.reshape(8, 128),
        lengths,
        counts,
        norm_gain,
        gate_weight,
        up_weight,
        down_weight,
    )


def solution(mesh):
    return jax.shard_map(
        on_device,
        mesh=mesh,
        in_specs=(
            P("attn", "ffn"),
            P("attn", "ffn"),
            P("attn", "ffn", None, None),
            P("attn", "ffn", None, None),
            P("attn", "ffn", None),
            P("attn", "ffn", None),
            P("attn"),
            P("attn"),
            P(),
            P("attn", "ffn"),
            P("attn", "ffn"),
            P("attn", "ffn"),
        ),
        out_specs=P("attn", "ffn"),
        check_vma=False,
    )
```

```python
import jax
import jax.numpy as jnp
from jax import lax
from jax.experimental import pallas as pl
from jax.experimental.pallas import tpu as pltpu
from jax.sharding import PartitionSpec as P

D = 8192


epsilon = 1e-05


MESH = pl.DeviceIdType.MESH
N = 8
NX = 4
HALF = 512
UNITS = 448
MAIN = 384
TILES = ((0, 256), (256, 256), (512, 256), (768, 128))
STEPS = (0, 1, -1, 2, -2, 3, -3, 4)
GROUPS = ((0, 1, 2, 3, 4), (5, 6, 7))


def transposed_dot(rows, weight):
    return lax.dot_general(rows, weight, (((1,), (1,)), ((), ())), preferred_element_type=jnp.float32)


def exchange(low, high):
    axis = low.ndim - 2
    upper = lax.broadcasted_iota(jnp.int32, low.shape, axis) < 4
    return jnp.where(upper, low, pltpu.roll(high, 4, axis)), jnp.where(upper, pltpu.roll(low, 4, axis), high)


def attend(
    inputs,
    queries_ref,
    keys_ref,
    values_ref,
    new_keys_ref,
    new_values_ref,
    lengths_ref,
    residual_ref,
    by_head,
    hidden_ref,
):
    for load in inputs[:4]:
        load.wait()
    score_scale = 1.0 / 128**0.5
    for h in range(8):
        by_head[h * 8 : h * 8 + 8, :] = queries_ref[:, h * 128 : h * 128 + 128].astype(jnp.float32)
    new_keys = new_keys_ref[...].astype(jnp.float32)
    position = lax.broadcasted_iota(jnp.int32, (8, 512), 1)
    scores = []
    own = []
    for r in range(8):
        query = by_head[pl.ds(r, 8, stride=8), :]
        own.append(jnp.sum(query * new_keys[r : r + 1, :], axis=1, keepdims=True))
        slot = transposed_dot(query.astype(jnp.bfloat16), keys_ref[r]) * score_scale
        scores.append(jnp.where(position < lengths_ref[r], slot, -1e30))
    scores = jnp.concatenate(scores, axis=0)
    own = jnp.concatenate(own, axis=0) * score_scale
    row_max = jnp.maximum(jnp.max(scores, axis=1, keepdims=True), own)
    key_weights = jnp.exp(scores - row_max)
    own_weight = jnp.exp(own - row_max)
    denominator = jnp.sum(key_weights, axis=1, keepdims=True) + own_weight
    key_probs = key_weights / denominator
    own_prob = (own_weight / denominator).astype(jnp.bfloat16).astype(jnp.float32)
    for load in inputs[4:]:
        load.wait()
    new_values = new_values_ref[...].astype(jnp.float32)
    for r in range(8):
        probs = key_probs[r * 8 : r * 8 + 8, :].astype(jnp.bfloat16)
        mixed = jnp.dot(probs, values_ref[r], preferred_element_type=jnp.float32)
        mixed = mixed + own_prob[r * 8 : r * 8 + 8, :] * new_values[r : r + 1, :]
        by_head[pl.ds(r, 8, stride=8), :] = mixed.astype(jnp.bfloat16).astype(jnp.float32)
    for h in range(8):
        lanes = slice(h * 128, h * 128 + 128)
        hidden = residual_ref[:, lanes].astype(jnp.float32) + by_head[h * 8 : h * 8 + 8, :]
        hidden_ref[:, lanes] = hidden.astype(jnp.bfloat16).astype(jnp.float32)


def kernel(
    residual_hbm,
    queries_hbm,
    keys_hbm,
    values_hbm,
    new_keys_hbm,
    new_values_hbm,
    lengths_hbm,
    counts_hbm,
    gain_hbm,
    gate_hbm,
    up_hbm,
    down_hbm,
    out_ref,
    residual_ref,
    queries_ref,
    keys_ref,
    values_ref,
    new_keys_ref,
    new_values_ref,
    lengths_ref,
    counts_ref,
    gain_ref,
    by_head,
    hidden_ref,
    gu,
    down,
    held,
    terms,
    back,
    onward,
    last,
    asem,
    wsem,
    g1s,
    g1r,
    g2s,
    g2r,
    r1s,
    r1r,
    r2s,
    r2r,
    *by_group,
):
    each = len(by_group) // len(GROUPS)
    by_group = [by_group[g * each : g * each + each] for g in range(len(GROUPS))]
    attn = lax.axis_index("attn")
    ffn = lax.axis_index("ffn")
    z, y = lax.div(attn, N), lax.rem(attn, N)
    x, c = lax.div(ffn, 2), lax.rem(ffn, 2)

    def at(zz, yy, xx, cc):
        return (zz * N + yy, xx * 2 + cc)

    def past(i, k, n):
        return lax.rem(i + k, n)

    inputs = [
        pltpu.make_async_copy(source, target, asem.at[i])
        for i, (source, target) in enumerate(
            (
                (queries_hbm, queries_ref),
                (new_keys_hbm, new_keys_ref),
                (lengths_hbm, lengths_ref),
                (keys_hbm, keys_ref),
                (values_hbm, values_ref),
                (new_values_hbm, new_values_ref),
                (residual_hbm, residual_ref),
                (counts_hbm, counts_ref),
                (gain_hbm.at[pl.ds(ffn * 1024, 1024)], gain_ref),
            )
        )
    ]
    for load in inputs:
        load.start()
    loads = [
        pltpu.make_async_copy(gate_hbm, gu.at[pl.ds(0, UNITS)], wsem.at[0]),
        pltpu.make_async_copy(up_hbm.at[pl.ds(MAIN, UNITS - MAIN)], gu.at[pl.ds(UNITS, UNITS - MAIN)], wsem.at[1]),
        pltpu.make_async_copy(up_hbm.at[pl.ds(0, MAIN)], gu.at[pl.ds(512, MAIN)], wsem.at[2]),
        pltpu.make_async_copy(down_hbm, down, wsem.at[3]),
    ]
    for load in loads:
        load.start()

    barrier = pltpu.get_barrier_semaphore()
    partners = [at(past(z, k, N), y, x, c) for k in range(1, N)]
    partners += [at(z, past(y, k, N), x, c) for k in range(1, N)]
    partners += [at(z, y, past(x, k, NX), c) for k in range(1, NX)]
    partners += [at(z, y, x, 1 - c)]
    for partner in partners:
        pl.semaphore_signal(barrier, inc=1, device_id=partner, device_id_type=MESH)

    attend(
        inputs,
        queries_ref,
        keys_ref,
        values_ref,
        new_keys_ref,
        new_values_ref,
        lengths_ref,
        residual_ref,
        by_head,
        hidden_ref,
    )
    gain = gain_ref[...].astype(jnp.float32).reshape(1, 1024)
    pl.semaphore_wait(barrier, len(partners))

    sent = []

    def send(source, target, send_sem, recv_sem, device):
        copy = pltpu.make_async_remote_copy(
            src_ref=source, dst_ref=target, send_sem=send_sem, recv_sem=recv_sem, device_id=device, device_id_type=MESH
        )
        copy.start()
        sent.append(copy)
        return copy

    other = at(z, y, x, 1 - c)

    def along(is_z, step):
        if is_z:
            return at(lax.rem(z + (N + step), N), y, x, c)
        return at(z, lax.rem(y + (N + step), N), x, c)

    blocks = exchange(hidden_ref[:, :HALF], hidden_ref[:, HALF:])
    first, second = [{}, {}], [{}, {}]
    for route in range(2):
        held[route, 0, 0] = blocks[route].astype(jnp.bfloat16)
    for i in (7, 5, 6, 3, 4, 1, 2):
        for route in range(2):
            first[route][i] = send(
                held.at[route, 0, 0],
                held.at[route, 0, i],
                g1s.at[route, i],
                g1r.at[route, i],
                along(route == 1, -STEPS[i]),
            )

    def pass_on(route, i, source, device, part):
        span = (pl.ds(0, 5), pl.ds(5, 3), slice(None))[part]
        second[route][i, part] = send(
            held.at[route, source, span],
            held.at[route, i, span],
            g2s.at[route, part % 2, i],
            g2r.at[route, part % 2, i],
            device,
        )

    for part, arrived in enumerate(((1, 2, 3, 4), (5, 6, 7))):
        for route in range(2):
            for i in arrived:
                first[route][i].wait_recv()
            for i in (3, 4):
                pass_on(route, i, 0, along(route == 0, -STEPS[i]), part)
    for route in range(2):
        for i in (1, 2):
            pass_on(route, i, 0, along(route == 0, -STEPS[i]), 2)
    for part in range(2):
        for route in range(2):
            second[route][3, part].wait_recv()
            second[route][4, part].wait_recv()
            pass_on(route, 7, 3 + c, along(route == 0, -2 + 4 * c), part)
            pass_on(route, 5, 3, along(route == 0, -1), part)
            pass_on(route, 6, 4, along(route == 0, 1), part)

    def multiply(g):
        xs, ssb, pair_out, pair_in, pair_ss, own = by_group[g][:6]
        places = GROUPS[g]
        count = len(places)
        lane = lax.broadcasted_iota(jnp.int32, (4, 8, 128), 2)
        row = lax.broadcasted_iota(jnp.int32, (4, 8, 128), 1)
        for route in range(2):
            squares = jnp.zeros((4, 1, 128), jnp.float32)
            for d, i in enumerate(places):
                for part in {1: (2,), 2: (2,), 5: (0, 1), 6: (0, 1), 7: (0, 1)}.get(i, ()):
                    second[route][i, part].wait_recv()
                packed = held[route, i].astype(jnp.float32).reshape(4, 2, 8, HALF)
                low, high = exchange(packed[:, 0], packed[:, 1])
                square = jnp.sum(low * low + high * high, axis=2, keepdims=True)
                squares = squares + jnp.sum(jnp.where(lane == row + 8 * d, square, 0.0), axis=1, keepdims=True)
                xs[route * 4 : route * 4 + 4, d, :, :HALF] = (low * gain[:, :HALF]).astype(jnp.bfloat16)
                xs[route * 4 : route * 4 + 4, d, :, HALF:] = (high * gain[:, HALF:]).astype(jnp.bfloat16)
            ssb[route * 4 : route * 4 + 4] = squares
        if g == 0:
            for load in loads:
                load.wait()
        rows = xs[pl.ds((1 - c) * 4, 4)].reshape(32 * count, 1024)
        for start, width in TILES:
            block = transposed_dot(rows, gu[start : start + width, :]).astype(jnp.bfloat16)
            pair_out[:, :, :, start : start + width] = block.reshape(4, count, 8, width)
        pair = [
            send(pair_out, pair_in, by_group[g][11].at[0], by_group[g][12].at[0], other),
            send(ssb.at[pl.ds((1 - c) * 4, 4)], pair_ss, by_group[g][11].at[1], by_group[g][12].at[1], other),
        ]
        rows = xs[pl.ds(c * 4, 4)].reshape(32 * count, 1024)
        for start, width in TILES:
            block = transposed_dot(rows, gu[start : start + width, :])
            own[:, :, :, start : start + width] = block.reshape(4, count, 8, width)
        return pair

    def cross(g, before):
        ssb, _, pair_in, pair_ss, own, x_out, x_in, x_ss_out, x_ss_in = by_group[g][1:10]
        xss, xsr = by_group[g][13:15]
        for copy in before:
            copy.wait_recv()
        copies = []
        for k in (2, 1, 3):
            xx = past(x, k, NX)
            x_out[k] = (own[xx] + pair_in[xx].astype(jnp.float32)).astype(jnp.bfloat16)
            x_ss_out[k] = ssb[c * 4 + xx] + pair_ss[xx]
            device = at(z, y, xx, c)
            copies.append(send(x_out.at[k], x_in.at[k], xss.at[0, k], xsr.at[0, k], device))
            copies.append(send(x_ss_out.at[k], x_ss_in.at[k], xss.at[1, k], xsr.at[1, k], device))
        return copies

    def activate(g, before):
        ssb, _, pair_in, pair_ss, own, _, x_in, _, x_ss_in, act = by_group[g][1:11]
        acs, acr, fws, fwr = by_group[g][15:19]
        count = len(GROUPS[g])
        total = own[x] + pair_in[x].astype(jnp.float32)
        squares = ssb[c * 4 + x] + pair_ss[x]
        for copy in before:
            copy.wait_recv()
        for k in range(1, NX):
            total = total + x_in[k].astype(jnp.float32)
            squares = squares + x_ss_in[k]
        total = total.reshape(8 * count, 896)
        lane = lax.broadcasted_iota(jnp.int32, (8 * count, 128), 1)
        row = lax.broadcasted_iota(jnp.int32, (8 * count, 128), 0)
        mean_square = jnp.sum(jnp.where(lane == row, squares, 0.0), axis=1, keepdims=True) / D
        total = total * lax.rsqrt(mean_square + epsilon)
        gate = total[:, :512]
        silu = gate / (1.0 + jnp.exp(-gate))
        mine = c * 4 + x
        main = (silu[:, :MAIN] * total[:, 512:]).astype(jnp.bfloat16)
        act[mine, :, :, :MAIN] = main.reshape(count, 8, MAIN)
        tail = (silu[:, MAIN:] * pltpu.roll(total[:, MAIN:512], 64, 1))[:, : UNITS - MAIN]
        act[mine, :, :, MAIN:] = tail.astype(jnp.bfloat16).reshape(count, 8, UNITS - MAIN)
        copies = []
        for k in (2, 1, 3):
            device = at(z, y, past(x, k, NX), c)
            copies.append(send(act.at[mine], act.at[mine], acs.at[k], acr.at[k], device))
        return copies, [send(act.at[mine], act.at[mine], fws.at[0], fwr.at[0], other)]

    def forward(g, before):
        act = by_group[g][10]
        fws, fwr = by_group[g][17:19]
        copies, passed = before
        for k, copy in zip((1, 3, 2), (copies[1], copies[2], copies[0])):
            copy.wait_recv()
            place = c * 4 + past(x, NX - k, NX)
            passed.append(send(act.at[place], act.at[place], fws.at[k], fwr.at[k], other))
        return passed

    reduced = [{}, {}]

    def lower(g, before):
        act = by_group[g][10]
        places = GROUPS[g]
        count = len(places)
        for copy in before:
            copy.wait_recv()
        rows = act[...].reshape(64 * count, UNITS)
        for start in (0, 256):
            quarters = [
                jnp.dot(rows, down[:, at_lane : at_lane + 256], preferred_element_type=jnp.float32)
                for at_lane in (start, start + HALF)
            ]
            halves = exchange(*[quarter.reshape(2, 4, count, 8, 256) for quarter in quarters])
            for route in range(2):
                for d, i in enumerate(places):
                    block = jnp.stack([half[route, :, d] for half in halves], axis=1)
                    terms[route, i, :, :, start : start + 256] = block.reshape(N, 8, 256).astype(jnp.bfloat16)
        for i in (1, 2) if g == 0 else (7, 5, 6):
            for route in range(2):
                step = {1: 1, 2: -1, 5: 1, 6: -1, 7: 2 - 4 * c}[i]
                add_up(route, i, along(route == 0, step))

    def add_up(route, i, device):
        reduced[route][i] = send(
            terms.at[route, i], back.at[route, i], r1s.at[route, i], r1r.at[route, i], device
        )

    def relay(route):
        for i in (5, 6, 7):
            reduced[route][i].wait_recv()
        straight, cut = terms[route, 3 + c].astype(jnp.float32), terms[route, 4 - c].astype(jnp.float32)
        straight = straight + back[route, 5 + c].astype(jnp.float32) + back[route, 7].astype(jnp.float32)
        cut = cut + back[route, 6 - c].astype(jnp.float32)
        terms[route, 3 + c] = straight.astype(jnp.bfloat16)
        terms[route, 4 - c] = cut.astype(jnp.bfloat16)
        for i in (3, 4):
            add_up(route, i, along(route == 0, STEPS[i]))

    pairs = multiply(0)
    across = [cross(0, pairs)]
    pairs = multiply(1)
    across.append(cross(1, pairs))
    spread = [activate(g, across[g]) for g in range(2)]
    passed = [forward(g, spread[g]) for g in range(2)]
    for g in range(2):
        lower(g, passed[g])
    for route in range(2):
        relay(route)

    final = [[], []]
    for route in range(2):
        added = terms[route, 0].astype(jnp.float32)
        for i in range(1, 5):
            reduced[route][i].wait_recv()
            added = added + back[route, i].astype(jnp.float32)
        onward[route] = added.astype(jnp.bfloat16)
        for i in (7, 5, 6, 3, 4, 1, 2):
            final[route].append(
                send(
                    onward.at[route, i],
                    last.at[route, i],
                    r2s.at[route, i],
                    r2r.at[route, i],
                    along(route == 1, STEPS[i]),
                )
            )
    sums = []
    for route in range(2):
        for copy in final[route]:
            copy.wait_recv()
        added = onward[route, 0].astype(jnp.float32)
        for i in range(1, N):
            added = added + last[route, i].astype(jnp.float32)
        sums.append(added)
    live = lax.broadcasted_iota(jnp.int32, (8, HALF), 0) < counts_ref[0]
    for half, part in enumerate(exchange(*sums)):
        lanes = slice(half * HALF, (half + 1) * HALF)
        out_ref[:, lanes] = jnp.where(live, hidden_ref[:, lanes] + part, 0.0).astype(jnp.bfloat16)
    for copy in sent:
        copy.wait_send()


def whole_layer(*operands):
    bf, f32 = jnp.bfloat16, jnp.float32
    dma = pltpu.SemaphoreType.DMA
    vmem = pltpu.VMEM
    return pl.pallas_call(
        kernel,
        out_shape=jax.ShapeDtypeStruct((8, 1024), bf),
        in_specs=[pl.BlockSpec(memory_space=pltpu.HBM)] * 12,
        out_specs=pl.BlockSpec(memory_space=vmem),
        scratch_shapes=[
            vmem((8, 1024), bf),
            vmem((8, 1024), bf),
            vmem((8, 512, 128), bf),
            vmem((8, 512, 128), bf),
            vmem((8, 128), bf),
            vmem((8, 128), bf),
            pltpu.SMEM((8,), jnp.int32),
            pltpu.SMEM((1,), jnp.int32),
            vmem((1024,), bf),
            vmem((64, 128), f32),
            vmem((8, 1024), f32),
            vmem((896, 1024), bf),
            vmem((UNITS, 1024), bf),
            vmem((2, N, N, 8, HALF), bf),
            vmem((2, N, N, 8, HALF), bf),
            vmem((2, N, N, 8, HALF), bf),
            vmem((2, N, 8, HALF), bf),
            vmem((2, N, 8, HALF), bf),
            dma((9,)),
            dma((4,)),
        ]
        + [dma((2, N))] * 2
        + [dma((2, 2, N))] * 2
        + [dma((2, N))] * 4
        + [
            shape
            for count in [len(places) for places in GROUPS]
            for shape in (
                vmem((N, count, 8, 1024), bf),
                vmem((N, 1, 128), f32),
                vmem((4, count, 8, 896), bf),
                vmem((4, count, 8, 896), bf),
                vmem((4, 1, 128), f32),
                vmem((4, count, 8, 896), f32),
                vmem((NX, count, 8, 896), bf),
                vmem((NX, count, 8, 896), bf),
                vmem((NX, 1, 128), f32),
                vmem((NX, 1, 128), f32),
                vmem((2 * NX, count, 8, UNITS), bf),
                dma((2,)),
                dma((2,)),
                dma((2, NX)),
                dma((2, NX)),
                dma((NX,)),
                dma((NX,)),
                dma((NX,)),
                dma((NX,)),
            )
        ],
        compiler_params=pltpu.CompilerParams(
            collective_id=0, has_side_effects=True, vmem_limit_bytes=60 * 1024 * 1024
        ),
        cost_estimate=pl.CostEstimate(flops=1_430_000_000, bytes_accessed=5_000_000, transcendentals=0),
        name="whole_layer",
    )(*operands)


def on_device(
    residual,
    queries,
    cache_keys,
    cache_values,
    new_keys,
    new_values,
    lengths,
    counts,
    norm_gain,
    gate_weight,
    up_weight,
    down_weight,
):
    return whole_layer(
        residual,
        queries,
        cache_keys.reshape(8, 512, 128),
        cache_values.reshape(8, 512, 128),
        new_keys.reshape(8, 128),
        new_values.reshape(8, 128),
        lengths,
        counts,
        norm_gain,
        gate_weight,
        up_weight,
        down_weight,
    )


def solution(mesh):
    return jax.shard_map(
        on_device,
        mesh=mesh,
        in_specs=(
            P("attn", "ffn"),
            P("attn", "ffn"),
            P("attn", "ffn", None, None),
            P("attn", "ffn", None, None),
            P("attn", "ffn", None),
            P("attn", "ffn", None),
            P("attn"),
            P("attn"),
            P(),
            P("attn", "ffn"),
            P("attn", "ffn"),
            P("attn", "ffn"),
        ),
        out_specs=P("attn", "ffn"),
        check_vma=False,
    )
```

```python
import jax
import jax.numpy as jnp
from jax import lax
from jax.experimental import pallas as pl
from jax.experimental.pallas import tpu as pltpu
from jax.sharding import PartitionSpec as P

D = 8192


epsilon = 1e-05


MESH = pl.DeviceIdType.MESH
N = 8
NX = 4
HALF = 512
UNITS = 448
MAIN = 384
TILES = ((0, 256), (256, 256), (512, 256), (768, 128))
STEPS = (0, 1, -1, 2, -2, 3, -3, 4)
SPANS = (slice(0, 5), slice(5, 8), slice(0, 8))
GROUPS = ((0, 1, 2, 3, 4), (5, 6, 7))


def transposed_dot(rows, weight):
    return lax.dot_general(rows, weight, (((1,), (1,)), ((), ())), preferred_element_type=jnp.float32)


def exchange(low, high):
    axis = low.ndim - 2
    upper = lax.broadcasted_iota(jnp.int32, low.shape, axis) < 4
    return jnp.where(upper, low, pltpu.roll(high, 4, axis)), jnp.where(upper, pltpu.roll(low, 4, axis), high)


def attend(
    inputs,
    queries_ref,
    keys_ref,
    values_ref,
    new_keys_ref,
    new_values_ref,
    lengths_ref,
    residual_ref,
    by_head,
    hidden_ref,
):
    for load in inputs[:4]:
        load.wait()
    score_scale = 1.0 / 128**0.5
    for h in range(8):
        by_head[h * 8 : h * 8 + 8, :] = queries_ref[:, h * 128 : h * 128 + 128].astype(jnp.float32)
    new_keys = new_keys_ref[...].astype(jnp.float32)
    position = lax.broadcasted_iota(jnp.int32, (8, 512), 1)
    scores = []
    own = []
    for r in range(8):
        query = by_head[pl.ds(r, 8, stride=8), :]
        own.append(jnp.sum(query * new_keys[r : r + 1, :], axis=1, keepdims=True))
        slot = transposed_dot(query.astype(jnp.bfloat16), keys_ref[r]) * score_scale
        scores.append(jnp.where(position < lengths_ref[r], slot, -1e30))
    scores = jnp.concatenate(scores, axis=0)
    own = jnp.concatenate(own, axis=0) * score_scale
    row_max = jnp.maximum(jnp.max(scores, axis=1, keepdims=True), own)
    key_weights = jnp.exp(scores - row_max)
    own_weight = jnp.exp(own - row_max)
    denominator = jnp.sum(key_weights, axis=1, keepdims=True) + own_weight
    key_probs = key_weights / denominator
    own_prob = (own_weight / denominator).astype(jnp.bfloat16).astype(jnp.float32)
    for load in inputs[4:]:
        load.wait()
    new_values = new_values_ref[...].astype(jnp.float32)
    for r in range(8):
        probs = key_probs[r * 8 : r * 8 + 8, :].astype(jnp.bfloat16)
        mixed = jnp.dot(probs, values_ref[r], preferred_element_type=jnp.float32)
        mixed = mixed + own_prob[r * 8 : r * 8 + 8, :] * new_values[r : r + 1, :]
        by_head[pl.ds(r, 8, stride=8), :] = mixed.astype(jnp.bfloat16).astype(jnp.float32)
    for h in range(8):
        lanes = slice(h * 128, h * 128 + 128)
        hidden = residual_ref[:, lanes].astype(jnp.float32) + by_head[h * 8 : h * 8 + 8, :]
        hidden_ref[:, lanes] = hidden.astype(jnp.bfloat16).astype(jnp.float32)


def kernel(
    residual_hbm,
    queries_hbm,
    keys_hbm,
    values_hbm,
    new_keys_hbm,
    new_values_hbm,
    lengths_hbm,
    gain_hbm,
    gate_hbm,
    up_hbm,
    down_hbm,
    out_ref,
    residual_ref,
    queries_ref,
    keys_ref,
    values_ref,
    new_keys_ref,
    new_values_ref,
    lengths_ref,
    gain_ref,
    by_head,
    hidden_ref,
    gu,
    down,
    held,
    terms,
    back,
    onward,
    last,
    asem,
    wsem,
    g1s,
    g1r,
    g2s,
    g2r,
    r1s,
    r1r,
    r2s,
    r2r,
    *by_group,
):
    each = len(by_group) // len(GROUPS)
    by_group = [by_group[g * each : g * each + each] for g in range(len(GROUPS))]
    attn = lax.axis_index("attn")
    ffn = lax.axis_index("ffn")
    z, y = lax.div(attn, N), lax.rem(attn, N)
    x, c = lax.div(ffn, 2), lax.rem(ffn, 2)

    def at(zz, yy, xx, cc):
        return (zz * N + yy, xx * 2 + cc)

    def past(i, k, n):
        return lax.rem(i + k, n)

    inputs = [
        pltpu.make_async_copy(source, target, asem.at[i])
        for i, (source, target) in enumerate(
            (
                (queries_hbm, queries_ref),
                (new_keys_hbm, new_keys_ref),
                (lengths_hbm, lengths_ref),
                (keys_hbm, keys_ref),
                (values_hbm, values_ref),
                (new_values_hbm, new_values_ref),
                (residual_hbm, residual_ref),
                (gain_hbm.at[pl.ds(ffn * 1024, 1024)], gain_ref),
            )
        )
    ]
    for load in inputs:
        load.start()
    loads = [
        pltpu.make_async_copy(gate_hbm, gu.at[pl.ds(0, UNITS)], wsem.at[0]),
        pltpu.make_async_copy(up_hbm.at[pl.ds(MAIN, UNITS - MAIN)], gu.at[pl.ds(UNITS, UNITS - MAIN)], wsem.at[1]),
        pltpu.make_async_copy(up_hbm.at[pl.ds(0, MAIN)], gu.at[pl.ds(512, MAIN)], wsem.at[2]),
        pltpu.make_async_copy(down_hbm, down, wsem.at[3]),
    ]
    for load in loads:
        load.start()

    barrier = pltpu.get_barrier_semaphore()
    partners = [at(past(z, k, N), y, x, c) for k in range(1, N)]
    partners += [at(z, past(y, k, N), x, c) for k in range(1, N)]
    partners += [at(z, y, past(x, k, NX), c) for k in range(1, NX)]
    partners += [at(z, y, x, 1 - c)]
    for partner in partners:
        pl.semaphore_signal(barrier, inc=1, device_id=partner, device_id_type=MESH)

    attend(
        inputs,
        queries_ref,
        keys_ref,
        values_ref,
        new_keys_ref,
        new_values_ref,
        lengths_ref,
        residual_ref,
        by_head,
        hidden_ref,
    )
    gain = gain_ref[...].astype(jnp.float32).reshape(1, 1024)
    pl.semaphore_wait(barrier, len(partners))

    sent = []

    def send(source, target, send_sem, recv_sem, device):
        copy = pltpu.make_async_remote_copy(
            src_ref=source, dst_ref=target, send_sem=send_sem, recv_sem=recv_sem, device_id=device, device_id_type=MESH
        )
        copy.start()
        sent.append(copy)
        return copy

    other = at(z, y, x, 1 - c)

    def along(is_z, step):
        if is_z:
            return at(lax.rem(z + (N + step), N), y, x, c)
        return at(z, lax.rem(y + (N + step), N), x, c)

    blocks = exchange(hidden_ref[:, :HALF], hidden_ref[:, HALF:])
    first, second = [{}, {}], [{}, {}]
    for route in range(2):
        held[route, 0, 0] = blocks[route].astype(jnp.bfloat16)
    for i in (7, 5, 6, 3, 4, 1, 2):
        for route in range(2):
            first[route][i] = send(
                held.at[route, 0, 0],
                held.at[route, 0, i],
                g1s.at[route, i],
                g1r.at[route, i],
                along(route == 1, -STEPS[i]),
            )

    def pass_on(route, i, source, device, part):
        span = SPANS[part]
        second[route][i, part] = send(
            held.at[route, source, span],
            held.at[route, i, span],
            g2s.at[route, part % 2, i],
            g2r.at[route, part % 2, i],
            device,
        )

    for part, arrived in enumerate(((1, 2, 3, 4), (5, 6, 7))):
        for route in range(2):
            for i in arrived:
                first[route][i].wait_recv()
            for i in (3, 4):
                pass_on(route, i, 0, along(route == 0, -STEPS[i]), part)
    for route in range(2):
        for i in (1, 2):
            pass_on(route, i, 0, along(route == 0, -STEPS[i]), 2)
    for part in range(2):
        for route in range(2):
            second[route][3, part].wait_recv()
            second[route][4, part].wait_recv()
            pass_on(route, 7, 3 + c, along(route == 0, -2 + 4 * c), part)
            pass_on(route, 5, 3, along(route == 0, -1), part)
            pass_on(route, 6, 4, along(route == 0, 1), part)

    def multiply(g):
        xs, ssb, pair_out, pair_in, pair_ss, own = by_group[g][:6]
        places = GROUPS[g]
        count = len(places)
        lane = lax.broadcasted_iota(jnp.int32, (4, 8, 128), 2)
        row = lax.broadcasted_iota(jnp.int32, (4, 8, 128), 1)
        for route in range(2):
            squares = jnp.zeros((4, 1, 128), jnp.float32)
            for d, i in enumerate(places):
                for part in {1: (2,), 2: (2,), 5: (0, 1), 6: (0, 1), 7: (0, 1)}.get(i, ()):
                    second[route][i, part].wait_recv()
                packed = held[route, i].astype(jnp.float32).reshape(4, 2, 8, HALF)
                low, high = exchange(packed[:, 0], packed[:, 1])
                square = jnp.sum(low * low + high * high, axis=2, keepdims=True)
                squares = squares + jnp.sum(jnp.where(lane == row + 8 * d, square, 0.0), axis=1, keepdims=True)
                xs[route * 4 : route * 4 + 4, d, :, :HALF] = (low * gain[:, :HALF]).astype(jnp.bfloat16)
                xs[route * 4 : route * 4 + 4, d, :, HALF:] = (high * gain[:, HALF:]).astype(jnp.bfloat16)
            ssb[route * 4 : route * 4 + 4] = squares
        if g == 0:
            for load in loads:
                load.wait()
        rows = xs[pl.ds((1 - c) * 4, 4)].reshape(32 * count, 1024)
        for start, width in TILES:
            block = transposed_dot(rows, gu[start : start + width, :]).astype(jnp.bfloat16)
            pair_out[:, :, :, start : start + width] = block.reshape(4, count, 8, width)
        pair = [
            send(pair_out, pair_in, by_group[g][11].at[0], by_group[g][12].at[0], other),
            send(ssb.at[pl.ds((1 - c) * 4, 4)], pair_ss, by_group[g][11].at[1], by_group[g][12].at[1], other),
        ]
        rows = xs[pl.ds(c * 4, 4)].reshape(32 * count, 1024)
        for start, width in TILES:
            block = transposed_dot(rows, gu[start : start + width, :])
            own[:, :, :, start : start + width] = block.reshape(4, count, 8, width)
        return pair

    def cross(g, before):
        ssb, _, pair_in, pair_ss, own, x_out, x_in, x_ss_out, x_ss_in = by_group[g][1:10]
        xss, xsr = by_group[g][13:15]
        for copy in before:
            copy.wait_recv()
        copies = []
        for k in (2, 1, 3):
            xx = past(x, k, NX)
            x_out[k] = (own[xx] + pair_in[xx].astype(jnp.float32)).astype(jnp.bfloat16)
            x_ss_out[k] = ssb[c * 4 + xx] + pair_ss[xx]
            device = at(z, y, xx, c)
            copies.append(send(x_out.at[k], x_in.at[k], xss.at[0, k], xsr.at[0, k], device))
            copies.append(send(x_ss_out.at[k], x_ss_in.at[k], xss.at[1, k], xsr.at[1, k], device))
        return copies

    def activate(g, before):
        ssb, _, pair_in, pair_ss, own, _, x_in, _, x_ss_in, act = by_group[g][1:11]
        acs, acr, fws, fwr = by_group[g][15:19]
        count = len(GROUPS[g])
        total = own[x] + pair_in[x].astype(jnp.float32)
        squares = ssb[c * 4 + x] + pair_ss[x]
        for copy in before:
            copy.wait_recv()
        for k in range(1, NX):
            total = total + x_in[k].astype(jnp.float32)
            squares = squares + x_ss_in[k]
        total = total.reshape(8 * count, 896)
        lane = lax.broadcasted_iota(jnp.int32, (8 * count, 128), 1)
        row = lax.broadcasted_iota(jnp.int32, (8 * count, 128), 0)
        mean_square = jnp.sum(jnp.where(lane == row, squares, 0.0), axis=1, keepdims=True) / D
        total = total * lax.rsqrt(mean_square + epsilon)
        gate = total[:, :512]
        silu = gate / (1.0 + jnp.exp(-gate))
        mine = c * 4 + x
        main = (silu[:, :MAIN] * total[:, 512:]).astype(jnp.bfloat16)
        act[mine, :, :, :MAIN] = main.reshape(count, 8, MAIN)
        tail = (silu[:, MAIN:] * pltpu.roll(total[:, MAIN:512], 64, 1))[:, : UNITS - MAIN]
        act[mine, :, :, MAIN:] = tail.astype(jnp.bfloat16).reshape(count, 8, UNITS - MAIN)
        copies = []
        for k in (2, 1, 3):
            device = at(z, y, past(x, k, NX), c)
            copies.append(send(act.at[mine], act.at[mine], acs.at[k], acr.at[k], device))
        return copies, [send(act.at[mine], act.at[mine], fws.at[0], fwr.at[0], other)]

    def forward(g, before):
        act = by_group[g][10]
        fws, fwr = by_group[g][17:19]
        copies, passed = before
        for k, copy in zip((1, 3, 2), (copies[1], copies[2], copies[0])):
            copy.wait_recv()
            place = c * 4 + past(x, NX - k, NX)
            passed.append(send(act.at[place], act.at[place], fws.at[k], fwr.at[k], other))
        return passed

    reduced = [{}, {}]

    def lower(g, before):
        act = by_group[g][10]
        places = GROUPS[g]
        count = len(places)
        for copy in before:
            copy.wait_recv()
        rows = act[...].reshape(64 * count, UNITS)
        for start in (0, 256):
            quarters = [
                jnp.dot(rows, down[:, at_lane : at_lane + 256], preferred_element_type=jnp.float32)
                for at_lane in (start, start + HALF)
            ]
            halves = exchange(*[quarter.reshape(2, 4, count, 8, 256) for quarter in quarters])
            for route in range(2):
                for d, i in enumerate(places):
                    block = jnp.stack([half[route, :, d] for half in halves], axis=1)
                    terms[route, i, :, :, start : start + 256] = block.reshape(N, 8, 256).astype(jnp.bfloat16)
        for part in (2,) if g == 0 else (1, 0):
            for i in (1, 2) if g == 0 else (7, 5, 6):
                for route in range(2):
                    step = {1: 1, 2: -1, 5: 1, 6: -1, 7: 2 - 4 * c}[i]
                    add_up(route, i, along(route == 0, step), part)

    def add_up(route, i, device, part):
        reduced[route][i, part] = send(
            terms.at[route, i, SPANS[part]],
            back.at[route, i, SPANS[part]],
            r1s.at[part % 2, route, i],
            r1r.at[part % 2, route, i],
            device,
        )

    def relay(route, part):
        for i in (5, 6, 7):
            reduced[route][i, part].wait_recv()
        span = SPANS[part]
        straight, cut = terms[route, 3 + c, span].astype(jnp.float32), terms[route, 4 - c, span].astype(jnp.float32)
        straight = straight + back[route, 5 + c, span].astype(jnp.float32) + back[route, 7, span].astype(jnp.float32)
        cut = cut + back[route, 6 - c, span].astype(jnp.float32)
        terms[route, 3 + c, span] = straight.astype(jnp.bfloat16)
        terms[route, 4 - c, span] = cut.astype(jnp.bfloat16)
        for i in (3, 4):
            add_up(route, i, along(route == 0, STEPS[i]), part)

    pairs = multiply(0)
    across = [cross(0, pairs)]
    pairs = multiply(1)
    across.append(cross(1, pairs))
    spread = [activate(g, across[g]) for g in range(2)]
    passed = [forward(g, spread[g]) for g in range(2)]
    for g in range(2):
        lower(g, passed[g])
    for part in (1, 0):
        for route in range(2):
            relay(route, part)

    final = [[], []]
    for part in (1, 0):
        span = SPANS[part]
        for route in range(2):
            if part:
                for i in (1, 2):
                    reduced[route][i, 2].wait_recv()
            for i in (3, 4):
                reduced[route][i, part].wait_recv()
            added = terms[route, 0, span].astype(jnp.float32)
            for i in range(1, 5):
                added = added + back[route, i, span].astype(jnp.float32)
            onward[route, span] = added.astype(jnp.bfloat16)
            for i in ((3, 4, 1, 2), (7, 5, 6))[part]:
                final[route].append(
                    send(
                        onward.at[route, i],
                        last.at[route, i],
                        r2s.at[route, i],
                        r2r.at[route, i],
                        along(route == 1, STEPS[i]),
                    )
                )
    sums = []
    for route in range(2):
        for copy in final[route]:
            copy.wait_recv()
        added = onward[route, 0].astype(jnp.float32)
        for i in range(1, N):
            added = added + last[route, i].astype(jnp.float32)
        sums.append(added)
    for half, part in enumerate(exchange(*sums)):
        lanes = slice(half * HALF, (half + 1) * HALF)
        out_ref[:, lanes] = (hidden_ref[:, lanes] + part).astype(jnp.bfloat16)
    for copy in sent:
        copy.wait_send()


def whole_layer(*operands):
    bf, f32 = jnp.bfloat16, jnp.float32
    dma = pltpu.SemaphoreType.DMA
    vmem = pltpu.VMEM
    return pl.pallas_call(
        kernel,
        out_shape=jax.ShapeDtypeStruct((8, 1024), bf),
        in_specs=[pl.BlockSpec(memory_space=pltpu.HBM)] * 11,
        out_specs=pl.BlockSpec(memory_space=vmem),
        scratch_shapes=[
            vmem((8, 1024), bf),
            vmem((8, 1024), bf),
            vmem((8, 512, 128), bf),
            vmem((8, 512, 128), bf),
            vmem((8, 128), bf),
            vmem((8, 128), bf),
            pltpu.SMEM((8,), jnp.int32),
            vmem((1024,), bf),
            vmem((64, 128), f32),
            vmem((8, 1024), f32),
            vmem((896, 1024), bf),
            vmem((UNITS, 1024), bf),
            vmem((2, N, N, 8, HALF), bf),
            vmem((2, N, N, 8, HALF), bf),
            vmem((2, N, N, 8, HALF), bf),
            vmem((2, N, 8, HALF), bf),
            vmem((2, N, 8, HALF), bf),
            dma((8,)),
            dma((4,)),
        ]
        + [dma((2, N))] * 2
        + [dma((2, 2, N))] * 4
        + [dma((2, N))] * 2
        + [
            shape
            for count in [len(places) for places in GROUPS]
            for shape in (
                vmem((N, count, 8, 1024), bf),
                vmem((N, 1, 128), f32),
                vmem((4, count, 8, 896), bf),
                vmem((4, count, 8, 896), bf),
                vmem((4, 1, 128), f32),
                vmem((4, count, 8, 896), f32),
                vmem((NX, count, 8, 896), bf),
                vmem((NX, count, 8, 896), bf),
                vmem((NX, 1, 128), f32),
                vmem((NX, 1, 128), f32),
                vmem((2 * NX, count, 8, UNITS), bf),
                dma((2,)),
                dma((2,)),
                dma((2, NX)),
                dma((2, NX)),
                dma((NX,)),
                dma((NX,)),
                dma((NX,)),
                dma((NX,)),
            )
        ],
        compiler_params=pltpu.CompilerParams(
            collective_id=0, has_side_effects=True, vmem_limit_bytes=60 * 1024 * 1024
        ),
        cost_estimate=pl.CostEstimate(flops=1_430_000_000, bytes_accessed=5_000_000, transcendentals=0),
        name="whole_layer",
    )(*operands)


def on_device(
    residual,
    queries,
    cache_keys,
    cache_values,
    new_keys,
    new_values,
    lengths,
    counts,
    norm_gain,
    gate_weight,
    up_weight,
    down_weight,
):
    result = whole_layer(
        residual,
        queries,
        cache_keys.reshape(8, 512, 128),
        cache_values.reshape(8, 512, 128),
        new_keys.reshape(8, 128),
        new_values.reshape(8, 128),
        lengths,
        norm_gain,
        gate_weight,
        up_weight,
        down_weight,
    )
    is_live = jnp.arange(8, dtype=jnp.int32) < counts[0]
    return jnp.where(is_live[:, None], result, jnp.zeros_like(result))


def solution(mesh):
    return jax.shard_map(
        on_device,
        mesh=mesh,
        in_specs=(
            P("attn", "ffn"),
            P("attn", "ffn"),
            P("attn", "ffn", None, None),
            P("attn", "ffn", None, None),
            P("attn", "ffn", None),
            P("attn", "ffn", None),
            P("attn"),
            P("attn"),
            P(),
            P("attn", "ffn"),
            P("attn", "ffn"),
            P("attn", "ffn"),
        ),
        out_specs=P("attn", "ffn"),
        check_vma=False,
    )
```

```python
import jax
import jax.numpy as jnp
from jax import lax
from jax.experimental import pallas as pl
from jax.experimental.pallas import tpu as pltpu
from jax.sharding import PartitionSpec as P

D = 8192


epsilon = 1e-05


MESH = pl.DeviceIdType.MESH
N = 8
NX = 4
WIDE = 1024
UNITS = 448
MAIN = 384
TILES = ((0, 256), (256, 256), (512, 256), (768, 128))
STEPS = (0, 1, -1, 2, -2, 3, -3, 4)
SPANS = (slice(0, 5), slice(5, 8), slice(0, 8))
GROUPS = ((0, 1, 2, 3, 4), (5, 6, 7))


def transposed_dot(rows, weight):
    return lax.dot_general(rows, weight, (((1,), (1,)), ((), ())), preferred_element_type=jnp.float32)


def exchange(low, high):
    axis = low.ndim - 2
    upper = lax.broadcasted_iota(jnp.int32, low.shape, axis) < 4
    return jnp.where(upper, low, pltpu.roll(high, 4, axis)), jnp.where(upper, pltpu.roll(low, 4, axis), high)


def attend(
    inputs,
    queries_ref,
    keys_ref,
    values_ref,
    new_keys_ref,
    new_values_ref,
    lengths_ref,
    residual_ref,
    by_head,
    hidden_ref,
):
    for load in inputs[:4]:
        load.wait()
    score_scale = 1.0 / 128**0.5
    for h in range(8):
        by_head[h * 8 : h * 8 + 8, :] = queries_ref[:, h * 128 : h * 128 + 128].astype(jnp.float32)
    new_keys = new_keys_ref[...].astype(jnp.float32)
    position = lax.broadcasted_iota(jnp.int32, (8, 512), 1)
    scores = []
    own = []
    for r in range(8):
        query = by_head[pl.ds(r, 8, stride=8), :]
        own.append(jnp.sum(query * new_keys[r : r + 1, :], axis=1, keepdims=True))
        slot = transposed_dot(query.astype(jnp.bfloat16), keys_ref[r]) * score_scale
        scores.append(jnp.where(position < lengths_ref[r], slot, -1e30))
    scores = jnp.concatenate(scores, axis=0)
    own = jnp.concatenate(own, axis=0) * score_scale
    row_max = jnp.maximum(jnp.max(scores, axis=1, keepdims=True), own)
    key_weights = jnp.exp(scores - row_max)
    own_weight = jnp.exp(own - row_max)
    denominator = jnp.sum(key_weights, axis=1, keepdims=True) + own_weight
    key_probs = key_weights / denominator
    own_prob = (own_weight / denominator).astype(jnp.bfloat16).astype(jnp.float32)
    for load in inputs[4:]:
        load.wait()
    new_values = new_values_ref[...].astype(jnp.float32)
    for r in range(8):
        probs = key_probs[r * 8 : r * 8 + 8, :].astype(jnp.bfloat16)
        mixed = jnp.dot(probs, values_ref[r], preferred_element_type=jnp.float32)
        mixed = mixed + own_prob[r * 8 : r * 8 + 8, :] * new_values[r : r + 1, :]
        by_head[pl.ds(r, 8, stride=8), :] = mixed.astype(jnp.bfloat16).astype(jnp.float32)
    for h in range(8):
        lanes = slice(h * 128, h * 128 + 128)
        hidden = residual_ref[:, lanes].astype(jnp.float32) + by_head[h * 8 : h * 8 + 8, :]
        hidden_ref[:, lanes] = hidden.astype(jnp.bfloat16).astype(jnp.float32)


def kernel(
    residual_hbm,
    queries_hbm,
    keys_hbm,
    values_hbm,
    new_keys_hbm,
    new_values_hbm,
    lengths_hbm,
    gain_hbm,
    gate_hbm,
    up_hbm,
    down_hbm,
    out_ref,
    residual_ref,
    queries_ref,
    keys_ref,
    values_ref,
    new_keys_ref,
    new_values_ref,
    lengths_ref,
    gain_ref,
    by_head,
    hidden_ref,
    gu,
    down,
    swap,
    held,
    terms,
    back,
    onward,
    last,
    result,
    asem,
    wsem,
    sws,
    swr,
    g1s,
    g1r,
    g2s,
    g2r,
    r1s,
    r1r,
    r2s,
    r2r,
    *by_group,
):
    each = len(by_group) // len(GROUPS)
    by_group = [by_group[g * each : g * each + each] for g in range(len(GROUPS))]
    attn = lax.axis_index("attn")
    ffn = lax.axis_index("ffn")
    z, y = lax.div(attn, N), lax.rem(attn, N)
    x, c = lax.div(ffn, 2), lax.rem(ffn, 2)

    def at(zz, yy, xx, cc):
        return (zz * N + yy, xx * 2 + cc)

    def past(i, k, n):
        return lax.rem(i + k, n)

    inputs = [
        pltpu.make_async_copy(source, target, asem.at[i])
        for i, (source, target) in enumerate(
            (
                (queries_hbm, queries_ref),
                (new_keys_hbm, new_keys_ref),
                (lengths_hbm, lengths_ref),
                (keys_hbm, keys_ref),
                (values_hbm, values_ref),
                (new_values_hbm, new_values_ref),
                (residual_hbm, residual_ref),
                (gain_hbm.at[pl.ds(x * 2048, 2048)], gain_ref),
            )
        )
    ]
    for load in inputs:
        load.start()
    loads = [
        pltpu.make_async_copy(gate_hbm, gu.at[c, pl.ds(0, UNITS)], wsem.at[0]),
        pltpu.make_async_copy(up_hbm.at[pl.ds(MAIN, UNITS - MAIN)], gu.at[c, pl.ds(UNITS, UNITS - MAIN)], wsem.at[1]),
        pltpu.make_async_copy(up_hbm.at[pl.ds(0, MAIN)], gu.at[c, pl.ds(512, MAIN)], wsem.at[2]),
        pltpu.make_async_copy(down_hbm, down.at[c], wsem.at[3]),
    ]
    for load in loads:
        load.start()

    barrier = pltpu.get_barrier_semaphore()
    partners = [at(past(z, k, N), y, x, c) for k in range(1, N)]
    partners += [at(z, past(y, k, N), x, c) for k in range(1, N)]
    partners += [at(z, y, past(x, k, NX), c) for k in range(1, NX)]
    partners += [at(z, y, x, 1 - c)]
    for partner in partners:
        pl.semaphore_signal(barrier, inc=1, device_id=partner, device_id_type=MESH)

    attend(
        inputs,
        queries_ref,
        keys_ref,
        values_ref,
        new_keys_ref,
        new_values_ref,
        lengths_ref,
        residual_ref,
        by_head,
        hidden_ref,
    )
    gain = gain_ref[...].astype(jnp.float32).reshape(1, 2048)
    swap[c] = hidden_ref[...].astype(jnp.bfloat16)
    pl.semaphore_wait(barrier, len(partners))

    sent = []

    def send(source, target, send_sem, recv_sem, device):
        copy = pltpu.make_async_remote_copy(
            src_ref=source, dst_ref=target, send_sem=send_sem, recv_sem=recv_sem, device_id=device, device_id_type=MESH
        )
        copy.start()
        sent.append(copy)
        return copy

    other = at(z, y, x, 1 - c)

    def along(second_axis, step):
        on_z = 1 - c if second_axis else c
        return at(lax.rem(z + N + step * on_z, N), lax.rem(y + N + step * (1 - on_z), N), x, c)

    swapped = [send(swap.at[c], swap.at[c], sws.at[0], swr.at[0], other)]
    for load in loads:
        load.wait()
    swapped[0].wait_recv()

    blocks = exchange(swap[0].astype(jnp.float32), swap[1].astype(jnp.float32))
    held[0, 0] = jnp.where(c == 0, blocks[0], blocks[1]).astype(jnp.bfloat16)
    first, second = {}, {}
    for i in (7, 5, 6, 3, 4, 1, 2):
        first[i] = send(held.at[0, 0], held.at[0, i], g1s.at[i], g1r.at[i], along(False, -STEPS[i]))
    swapped.append(send(gu.at[c], gu.at[c], sws.at[1], swr.at[1], other))
    swapped.append(send(down.at[c], down.at[c], sws.at[2], swr.at[2], other))

    def pass_on(i, source, step, part):
        span = SPANS[part]
        second[i, part] = send(
            held.at[source, span],
            held.at[i, span],
            g2s.at[part % 2, i],
            g2r.at[part % 2, i],
            along(True, step),
        )

    for part, arrived in enumerate(((1, 2, 3, 4), (5, 6, 7))):
        for i in arrived:
            first[i].wait_recv()
        for i in (3, 4):
            pass_on(i, 0, -STEPS[i], part)
    for i in (1, 2):
        pass_on(i, 0, -STEPS[i], 2)
    for part in range(2):
        second[3, part].wait_recv()
        second[4, part].wait_recv()
        pass_on(7, 3 + part, -2 + 4 * part, part)
        pass_on(5, 3, -1, part)
        pass_on(6, 4, 1, part)

    def multiply(g):
        xs, ssb, own = by_group[g][:3]
        places = GROUPS[g]
        count = len(places)
        lane = lax.broadcasted_iota(jnp.int32, (4, 8, 128), 2)
        row = lax.broadcasted_iota(jnp.int32, (4, 8, 128), 1)
        squares = jnp.zeros((4, 1, 128), jnp.float32)
        for d, i in enumerate(places):
            for part in {1: (2,), 2: (2,), 5: (0, 1), 6: (0, 1), 7: (0, 1)}.get(i, ()):
                second[i, part].wait_recv()
            packed = held[i].astype(jnp.float32).reshape(4, 2, 8, WIDE)
            low, high = exchange(packed[:, 0], packed[:, 1])
            square = jnp.sum(low * low + high * high, axis=2, keepdims=True)
            squares = squares + jnp.sum(jnp.where(lane == row + 8 * d, square, 0.0), axis=1, keepdims=True)
            xs[0, :, d] = (low * gain[:, :WIDE]).astype(jnp.bfloat16)
            xs[1, :, d] = (high * gain[:, WIDE:]).astype(jnp.bfloat16)
        ssb[...] = squares
        if g == 0:
            swapped[1].wait_recv()
        rows = [xs[core].reshape(32 * count, WIDE) for core in range(2)]
        for start, width in TILES:
            block = transposed_dot(rows[0], gu[0, start : start + width, :])
            block = block + transposed_dot(rows[1], gu[1, start : start + width, :])
            own[:, :, :, start : start + width] = block.reshape(4, count, 8, width)

    def cross(g):
        ssb, own, x_out, x_in, x_ss_out, x_ss_in = by_group[g][1:7]
        xss, xsr = by_group[g][8:10]
        copies = []
        for k in (2, 1, 3):
            xx = past(x, k, NX)
            x_out[k] = own[xx].astype(jnp.bfloat16)
            x_ss_out[k] = ssb[xx]
            device = at(z, y, xx, c)
            copies.append(send(x_out.at[k], x_in.at[k], xss.at[0, k], xsr.at[0, k], device))
            copies.append(send(x_ss_out.at[k], x_ss_in.at[k], xss.at[1, k], xsr.at[1, k], device))
        return copies

    def activate(g, before):
        ssb, own, _, x_in, _, x_ss_in, act = by_group[g][1:8]
        acs, acr = by_group[g][10:12]
        count = len(GROUPS[g])
        total = own[x]
        squares = ssb[x]
        for copy in before:
            copy.wait_recv()
        for k in range(1, NX):
            total = total + x_in[k].astype(jnp.float32)
            squares = squares + x_ss_in[k]
        total = total.reshape(8 * count, 896)
        lane = lax.broadcasted_iota(jnp.int32, (8 * count, 128), 1)
        row = lax.broadcasted_iota(jnp.int32, (8 * count, 128), 0)
        mean_square = jnp.sum(jnp.where(lane == row, squares, 0.0), axis=1, keepdims=True) / D
        total = total * lax.rsqrt(mean_square + epsilon)
        gate = total[:, :512]
        silu = gate / (1.0 + jnp.exp(-gate))
        main = (silu[:, :MAIN] * total[:, 512:]).astype(jnp.bfloat16)
        act[x, :, :, :MAIN] = main.reshape(count, 8, MAIN)
        tail = (silu[:, MAIN:] * pltpu.roll(total[:, MAIN:512], 64, 1))[:, : UNITS - MAIN]
        act[x, :, :, MAIN:] = tail.astype(jnp.bfloat16).reshape(count, 8, UNITS - MAIN)
        copies = []
        for k in (2, 1, 3):
            device = at(z, y, past(x, k, NX), c)
            copies.append(send(act.at[x], act.at[x], acs.at[k], acr.at[k], device))
        return copies

    reduced = {}

    def lower(g, before):
        act = by_group[g][7]
        places = GROUPS[g]
        count = len(places)
        for copy in before:
            copy.wait_recv()
        if g == 0:
            swapped[2].wait_recv()
        rows = act[...].reshape(32 * count, UNITS)
        for start in range(0, WIDE, 256):
            quarters = [
                jnp.dot(rows, down[core, :, start : start + 256], preferred_element_type=jnp.float32)
                for core in range(2)
            ]
            halves = exchange(*[quarter.reshape(4, count, 8, 256) for quarter in quarters])
            for d, i in enumerate(places):
                block = jnp.stack([half[:, d] for half in halves], axis=1)
                terms[i, :, :, start : start + 256] = block.reshape(N, 8, 256).astype(jnp.bfloat16)
        for part in (2,) if g == 0 else (1, 0):
            for i in (1, 2) if g == 0 else (7, 5, 6):
                add_up(i, {1: 1, 2: -1, 5: 1, 6: -1, 7: 2 - 4 * part}[i], part)

    def add_up(i, step, part):
        reduced[i, part] = send(
            terms.at[i, SPANS[part]],
            back.at[i, SPANS[part]],
            r1s.at[part % 2, i],
            r1r.at[part % 2, i],
            along(True, step),
        )

    def relay(part):
        for i in (5, 6, 7):
            reduced[i, part].wait_recv()
        span = SPANS[part]
        straight, cut = terms[3 + part, span].astype(jnp.float32), terms[4 - part, span].astype(jnp.float32)
        straight = straight + back[5 + part, span].astype(jnp.float32) + back[7, span].astype(jnp.float32)
        cut = cut + back[6 - part, span].astype(jnp.float32)
        terms[3 + part, span] = straight.astype(jnp.bfloat16)
        terms[4 - part, span] = cut.astype(jnp.bfloat16)
        for i in (3, 4):
            add_up(i, STEPS[i], part)

    across = []
    for g in range(2):
        multiply(g)
        across.append(cross(g))
    spread = [activate(g, across[g]) for g in range(2)]
    for g in range(2):
        lower(g, spread[g])
    for part in (1, 0):
        relay(part)

    final = []
    for part in (1, 0):
        span = SPANS[part]
        if part:
            for i in (1, 2):
                reduced[i, 2].wait_recv()
        for i in (3, 4):
            reduced[i, part].wait_recv()
        added = terms[0, span].astype(jnp.float32)
        for i in range(1, 5):
            added = added + back[i, span].astype(jnp.float32)
        onward[span] = added.astype(jnp.bfloat16)
        for i in ((3, 4, 1, 2), (7, 5, 6))[part]:
            final.append(send(onward.at[i], last.at[i], r2s.at[i], r2r.at[i], along(False, STEPS[i])))
    for copy in final:
        copy.wait_recv()
    added = onward[0].astype(jnp.float32)
    for i in range(1, N):
        added = added + last[i].astype(jnp.float32)
    result[c] = added
    send(result.at[c], result.at[c], sws.at[3], swr.at[3], other).wait_recv()
    low, high = exchange(result[0], result[1])
    out_ref[...] = (hidden_ref[...] + jnp.where(c == 0, low, high)).astype(jnp.bfloat16)
    for copy in sent:
        copy.wait_send()


def whole_layer(*operands):
    bf, f32 = jnp.bfloat16, jnp.float32
    dma = pltpu.SemaphoreType.DMA
    vmem = pltpu.VMEM
    return pl.pallas_call(
        kernel,
        out_shape=jax.ShapeDtypeStruct((8, 1024), bf),
        in_specs=[pl.BlockSpec(memory_space=pltpu.HBM)] * 11,
        out_specs=pl.BlockSpec(memory_space=vmem),
        scratch_shapes=[
            vmem((8, 1024), bf),
            vmem((8, 1024), bf),
            vmem((8, 512, 128), bf),
            vmem((8, 512, 128), bf),
            vmem((8, 128), bf),
            vmem((8, 128), bf),
            pltpu.SMEM((8,), jnp.int32),
            vmem((2048,), bf),
            vmem((64, 128), f32),
            vmem((8, 1024), f32),
            vmem((2, 896, WIDE), bf),
            vmem((2, UNITS, WIDE), bf),
            vmem((2, 8, WIDE), bf),
            vmem((N, N, 8, WIDE), bf),
            vmem((N, N, 8, WIDE), bf),
            vmem((N, N, 8, WIDE), bf),
            vmem((N, 8, WIDE), bf),
            vmem((N, 8, WIDE), bf),
            vmem((2, 8, WIDE), f32),
            dma((8,)),
            dma((4,)),
            dma((4,)),
            dma((4,)),
        ]
        + [dma((N,))] * 2
        + [dma((2, N))] * 4
        + [dma((N,))] * 2
        + [
            shape
            for count in [len(places) for places in GROUPS]
            for shape in (
                vmem((2, 4, count, 8, WIDE), bf),
                vmem((4, 1, 128), f32),
                vmem((4, count, 8, 896), f32),
                vmem((NX, count, 8, 896), bf),
                vmem((NX, count, 8, 896), bf),
                vmem((NX, 1, 128), f32),
                vmem((NX, 1, 128), f32),
                vmem((NX, count, 8, UNITS), bf),
                dma((2, NX)),
                dma((2, NX)),
                dma((NX,)),
                dma((NX,)),
            )
        ],
        compiler_params=pltpu.CompilerParams(
            collective_id=0, has_side_effects=True, vmem_limit_bytes=60 * 1024 * 1024
        ),
        cost_estimate=pl.CostEstimate(flops=1_430_000_000, bytes_accessed=5_000_000, transcendentals=0),
        name="whole_layer",
    )(*operands)


def on_device(
    residual,
    queries,
    cache_keys,
    cache_values,
    new_keys,
    new_values,
    lengths,
    counts,
    norm_gain,
    gate_weight,
    up_weight,
    down_weight,
):
    result = whole_layer(
        residual,
        queries,
        cache_keys.reshape(8, 512, 128),
        cache_values.reshape(8, 512, 128),
        new_keys.reshape(8, 128),
        new_values.reshape(8, 128),
        lengths,
        norm_gain,
        gate_weight,
        up_weight,
        down_weight,
    )
    is_live = jnp.arange(8, dtype=jnp.int32) < counts[0]
    return jnp.where(is_live[:, None], result, jnp.zeros_like(result))


def solution(mesh):
    return jax.shard_map(
        on_device,
        mesh=mesh,
        in_specs=(
            P("attn", "ffn"),
            P("attn", "ffn"),
            P("attn", "ffn", None, None),
            P("attn", "ffn", None, None),
            P("attn", "ffn", None),
            P("attn", "ffn", None),
            P("attn"),
            P("attn"),
            P(),
            P("attn", "ffn"),
            P("attn", "ffn"),
            P("attn", "ffn"),
        ),
        out_specs=P("attn", "ffn"),
        check_vma=False,
    )
```

```python
import jax
import jax.numpy as jnp
from jax import lax
from jax.experimental import pallas as pl
from jax.experimental.pallas import tpu as pltpu
from jax.sharding import PartitionSpec as P

D = 8192


epsilon = 1e-05


MESH = pl.DeviceIdType.MESH
N = 8
NX = 4
HALF = 512
UNITS = 448
MAIN = 384
TILES = ((0, 256), (256, 256), (512, 256), (768, 128))
STEPS = (0, 1, -1, 2, -2, 3, -3, 4)
SPANS = (slice(0, 5), slice(5, 8), slice(0, 8))
GROUPS = ((0, 1, 2, 3, 4), (5, 6, 7))


def transposed_dot(rows, weight):
    return lax.dot_general(rows, weight, (((1,), (1,)), ((), ())), preferred_element_type=jnp.float32)


def exchange(low, high):
    axis = low.ndim - 2
    upper = lax.broadcasted_iota(jnp.int32, low.shape, axis) < 4
    return jnp.where(upper, low, pltpu.roll(high, 4, axis)), jnp.where(upper, pltpu.roll(low, 4, axis), high)


def attend(
    inputs,
    queries_ref,
    keys_ref,
    values_ref,
    new_keys_ref,
    new_values_ref,
    lengths_ref,
    residual_ref,
    by_head,
    hidden_ref,
):
    for load in inputs[:4]:
        load.wait()
    score_scale = 1.0 / 128**0.5
    for h in range(8):
        by_head[h * 8 : h * 8 + 8, :] = queries_ref[:, h * 128 : h * 128 + 128].astype(jnp.float32)
    new_keys = new_keys_ref[...].astype(jnp.float32)
    position = lax.broadcasted_iota(jnp.int32, (8, 512), 1)
    scores = []
    own = []
    for r in range(8):
        query = by_head[pl.ds(r, 8, stride=8), :]
        own.append(jnp.sum(query * new_keys[r : r + 1, :], axis=1, keepdims=True))
        slot = transposed_dot(query.astype(jnp.bfloat16), keys_ref[r]) * score_scale
        scores.append(jnp.where(position < lengths_ref[r], slot, -1e30))
    scores = jnp.concatenate(scores, axis=0)
    own = jnp.concatenate(own, axis=0) * score_scale
    row_max = jnp.maximum(jnp.max(scores, axis=1, keepdims=True), own)
    key_weights = jnp.exp(scores - row_max)
    own_weight = jnp.exp(own - row_max)
    denominator = jnp.sum(key_weights, axis=1, keepdims=True) + own_weight
    key_probs = key_weights / denominator
    own_prob = (own_weight / denominator).astype(jnp.bfloat16).astype(jnp.float32)
    for load in inputs[4:]:
        load.wait()
    new_values = new_values_ref[...].astype(jnp.float32)
    for r in range(8):
        probs = key_probs[r * 8 : r * 8 + 8, :].astype(jnp.bfloat16)
        mixed = jnp.dot(probs, values_ref[r], preferred_element_type=jnp.float32)
        mixed = mixed + own_prob[r * 8 : r * 8 + 8, :] * new_values[r : r + 1, :]
        by_head[pl.ds(r, 8, stride=8), :] = mixed.astype(jnp.bfloat16).astype(jnp.float32)
    for h in range(8):
        lanes = slice(h * 128, h * 128 + 128)
        hidden = residual_ref[:, lanes].astype(jnp.float32) + by_head[h * 8 : h * 8 + 8, :]
        hidden_ref[:, lanes] = hidden.astype(jnp.bfloat16).astype(jnp.float32)


def kernel(
    residual_hbm,
    queries_hbm,
    keys_hbm,
    values_hbm,
    new_keys_hbm,
    new_values_hbm,
    lengths_hbm,
    gain_hbm,
    gate_hbm,
    up_hbm,
    down_hbm,
    out_ref,
    residual_ref,
    queries_ref,
    keys_ref,
    values_ref,
    new_keys_ref,
    new_values_ref,
    lengths_ref,
    gain_ref,
    by_head,
    hidden_ref,
    gu,
    down,
    held,
    terms,
    back,
    onward,
    last,
    asem,
    wsem,
    g1s,
    g1r,
    g2s,
    g2r,
    r1s,
    r1r,
    r2s,
    r2r,
    *by_group,
):
    each = len(by_group) // len(GROUPS)
    by_group = [by_group[g * each : g * each + each] for g in range(len(GROUPS))]
    attn = lax.axis_index("attn")
    ffn = lax.axis_index("ffn")
    z, y = lax.div(attn, N), lax.rem(attn, N)
    x, c = lax.div(ffn, 2), lax.rem(ffn, 2)

    def at(zz, yy, xx, cc):
        return (zz * N + yy, xx * 2 + cc)

    def past(i, k, n):
        return lax.rem(i + k, n)

    inputs = [
        pltpu.make_async_copy(source, target, asem.at[i])
        for i, (source, target) in enumerate(
            (
                (queries_hbm, queries_ref),
                (new_keys_hbm, new_keys_ref),
                (lengths_hbm, lengths_ref),
                (keys_hbm, keys_ref),
                (values_hbm, values_ref),
                (new_values_hbm, new_values_ref),
                (residual_hbm, residual_ref),
                (gain_hbm.at[pl.ds(ffn * 1024, 1024)], gain_ref),
            )
        )
    ]
    for load in inputs:
        load.start()
    loads = [
        pltpu.make_async_copy(gate_hbm, gu.at[pl.ds(0, UNITS)], wsem.at[0]),
        pltpu.make_async_copy(up_hbm.at[pl.ds(MAIN, UNITS - MAIN)], gu.at[pl.ds(UNITS, UNITS - MAIN)], wsem.at[1]),
        pltpu.make_async_copy(up_hbm.at[pl.ds(0, MAIN)], gu.at[pl.ds(512, MAIN)], wsem.at[2]),
        pltpu.make_async_copy(down_hbm, down, wsem.at[3]),
    ]
    for load in loads:
        load.start()

    barrier = pltpu.get_barrier_semaphore()
    partners = [at(past(z, k, N), y, x, c) for k in range(1, N)]
    partners += [at(z, past(y, k, N), x, c) for k in range(1, N)]
    partners += [at(z, y, past(x, k, NX), core) for k in range(1, NX) for core in (c, 1 - c)]
    partners += [at(z, y, x, 1 - c)]
    for partner in partners:
        pl.semaphore_signal(barrier, inc=1, device_id=partner, device_id_type=MESH)

    attend(
        inputs,
        queries_ref,
        keys_ref,
        values_ref,
        new_keys_ref,
        new_values_ref,
        lengths_ref,
        residual_ref,
        by_head,
        hidden_ref,
    )
    gain = gain_ref[...].astype(jnp.float32).reshape(1, 1024)
    pl.semaphore_wait(barrier, len(partners))

    sent = []

    def send(source, target, send_sem, recv_sem, device):
        copy = pltpu.make_async_remote_copy(
            src_ref=source, dst_ref=target, send_sem=send_sem, recv_sem=recv_sem, device_id=device, device_id_type=MESH
        )
        copy.start()
        sent.append(copy)
        return copy

    other = at(z, y, x, 1 - c)

    def along(is_z, step):
        if is_z:
            return at(lax.rem(z + (N + step), N), y, x, c)
        return at(z, lax.rem(y + (N + step), N), x, c)

    blocks = exchange(hidden_ref[:, :HALF], hidden_ref[:, HALF:])
    first, second = [{}, {}], [{}, {}]
    for route in range(2):
        held[route, 0, 0] = blocks[route].astype(jnp.bfloat16)
    for i in (7, 5, 6, 3, 4, 1, 2):
        for route in range(2):
            first[route][i] = send(
                held.at[route, 0, 0],
                held.at[route, 0, i],
                g1s.at[route, i],
                g1r.at[route, i],
                along(route == 1, -STEPS[i]),
            )

    def pass_on(route, i, source, device, part):
        span = SPANS[part]
        second[route][i, part] = send(
            held.at[route, source, span],
            held.at[route, i, span],
            g2s.at[route, part % 2, i],
            g2r.at[route, part % 2, i],
            device,
        )

    for part, arrived in enumerate(((1, 2, 3, 4), (5, 6, 7))):
        for route in range(2):
            for i in arrived:
                first[route][i].wait_recv()
            for i in (3, 4):
                pass_on(route, i, 0, along(route == 0, -STEPS[i]), part)
    for route in range(2):
        for i in (1, 2):
            pass_on(route, i, 0, along(route == 0, -STEPS[i]), 2)
    for part in range(2):
        for route in range(2):
            second[route][3, part].wait_recv()
            second[route][4, part].wait_recv()
            pass_on(route, 7, 3 + c, along(route == 0, -2 + 4 * c), part)
            pass_on(route, 5, 3, along(route == 0, -1), part)
            pass_on(route, 6, 4, along(route == 0, 1), part)

    def multiply(g):
        xs, ssb, pair_out, pair_in, pair_ss, own = by_group[g][:6]
        places = GROUPS[g]
        count = len(places)
        lane = lax.broadcasted_iota(jnp.int32, (4, 8, 128), 2)
        row = lax.broadcasted_iota(jnp.int32, (4, 8, 128), 1)
        for route in range(2):
            squares = jnp.zeros((4, 1, 128), jnp.float32)
            for d, i in enumerate(places):
                for part in {1: (2,), 2: (2,), 5: (0, 1), 6: (0, 1), 7: (0, 1)}.get(i, ()):
                    second[route][i, part].wait_recv()
                packed = held[route, i].astype(jnp.float32).reshape(4, 2, 8, HALF)
                low, high = exchange(packed[:, 0], packed[:, 1])
                square = jnp.sum(low * low + high * high, axis=2, keepdims=True)
                squares = squares + jnp.sum(jnp.where(lane == row + 8 * d, square, 0.0), axis=1, keepdims=True)
                xs[route * 4 : route * 4 + 4, d, :, :HALF] = (low * gain[:, :HALF]).astype(jnp.bfloat16)
                xs[route * 4 : route * 4 + 4, d, :, HALF:] = (high * gain[:, HALF:]).astype(jnp.bfloat16)
            ssb[route * 4 : route * 4 + 4] = squares
        if g == 0:
            for load in loads:
                load.wait()
        rows = xs[pl.ds((1 - c) * 4, 4)].reshape(32 * count, 1024)
        for start, width in TILES:
            block = transposed_dot(rows, gu[start : start + width, :]).astype(jnp.bfloat16)
            pair_out[:, :, :, start : start + width] = block.reshape(4, count, 8, width)
        pair = [
            send(pair_out, pair_in, by_group[g][11].at[0], by_group[g][12].at[0], other),
            send(ssb.at[pl.ds((1 - c) * 4, 4)], pair_ss, by_group[g][11].at[1], by_group[g][12].at[1], other),
        ]
        rows = xs[pl.ds(c * 4, 4)].reshape(32 * count, 1024)
        for start, width in TILES:
            block = transposed_dot(rows, gu[start : start + width, :])
            own[:, :, :, start : start + width] = block.reshape(4, count, 8, width)
        return pair

    def cross(g, before):
        ssb, _, pair_in, pair_ss, own, x_out, x_in, x_ss_out, x_ss_in = by_group[g][1:10]
        xss, xsr = by_group[g][13:15]
        for copy in before:
            copy.wait_recv()
        copies = []
        for k in (2, 1, 3):
            xx = past(x, k, NX)
            x_out[k] = (own[xx] + pair_in[xx].astype(jnp.float32)).astype(jnp.bfloat16)
            x_ss_out[k] = ssb[c * 4 + xx] + pair_ss[xx]
            device = at(z, y, xx, c)
            copies.append(send(x_out.at[k], x_in.at[k], xss.at[0, k], xsr.at[0, k], device))
            copies.append(send(x_ss_out.at[k], x_ss_in.at[k], xss.at[1, k], xsr.at[1, k], device))
        return copies

    def activate(g, before):
        ssb, _, pair_in, pair_ss, own, _, x_in, _, x_ss_in, act = by_group[g][1:11]
        acs, acr, fws, fwr = by_group[g][15:19]
        count = len(GROUPS[g])
        total = own[x] + pair_in[x].astype(jnp.float32)
        squares = ssb[c * 4 + x] + pair_ss[x]
        for copy in before:
            copy.wait_recv()
        for k in range(1, NX):
            total = total + x_in[k].astype(jnp.float32)
            squares = squares + x_ss_in[k]
        total = total.reshape(8 * count, 896)
        lane = lax.broadcasted_iota(jnp.int32, (8 * count, 128), 1)
        row = lax.broadcasted_iota(jnp.int32, (8 * count, 128), 0)
        mean_square = jnp.sum(jnp.where(lane == row, squares, 0.0), axis=1, keepdims=True) / D
        total = total * lax.rsqrt(mean_square + epsilon)
        gate = total[:, :512]
        silu = gate / (1.0 + jnp.exp(-gate))
        mine = c * 4 + x
        main = (silu[:, :MAIN] * total[:, 512:]).astype(jnp.bfloat16)
        act[mine, :, :, :MAIN] = main.reshape(count, 8, MAIN)
        tail = (silu[:, MAIN:] * pltpu.roll(total[:, MAIN:512], 64, 1))[:, : UNITS - MAIN]
        act[mine, :, :, MAIN:] = tail.astype(jnp.bfloat16).reshape(count, 8, UNITS - MAIN)
        copies = []
        for k in (2, 1, 3):
            device = at(z, y, past(x, k, NX), c)
            copies.append(send(act.at[mine], act.at[mine], acs.at[k], acr.at[k], device))
        passed = [send(act.at[mine], act.at[mine], fws.at[0], fwr.at[0], other)]
        if g == 1:
            for k in (2, 1, 3):
                device = at(z, y, past(x, k, NX), 1 - c)
                passed.append(send(act.at[mine], act.at[mine], fws.at[k], fwr.at[k], device))
        return copies, passed

    def forward(g, before):
        act = by_group[g][10]
        fws, fwr = by_group[g][17:19]
        copies, passed = before
        if g == 1:
            return copies + passed
        for k, copy in zip((1, 3, 2), (copies[1], copies[2], copies[0])):
            copy.wait_recv()
            place = c * 4 + past(x, NX - k, NX)
            passed.append(send(act.at[place], act.at[place], fws.at[k], fwr.at[k], other))
        return passed

    reduced = [{}, {}]

    def lower(g, before):
        act = by_group[g][10]
        places = GROUPS[g]
        count = len(places)
        for copy in before:
            copy.wait_recv()
        rows = act[...].reshape(64 * count, UNITS)
        for start in (0, 256):
            quarters = [
                jnp.dot(rows, down[:, at_lane : at_lane + 256], preferred_element_type=jnp.float32)
                for at_lane in (start, start + HALF)
            ]
            halves = exchange(*[quarter.reshape(2, 4, count, 8, 256) for quarter in quarters])
            for route in range(2):
                for d, i in enumerate(places):
                    block = jnp.stack([half[route, :, d] for half in halves], axis=1)
                    terms[route, i, :, :, start : start + 256] = block.reshape(N, 8, 256).astype(jnp.bfloat16)
        for part in (2,) if g == 0 else (1, 0):
            for i in (1, 2) if g == 0 else (7, 5, 6):
                for route in range(2):
                    step = {1: 1, 2: -1, 5: 1, 6: -1, 7: 2 - 4 * c}[i]
                    add_up(route, i, along(route == 0, step), part)

    def add_up(route, i, device, part):
        reduced[route][i, part] = send(
            terms.at[route, i, SPANS[part]],
            back.at[route, i, SPANS[part]],
            r1s.at[part % 2, route, i],
            r1r.at[part % 2, route, i],
            device,
        )

    def relay(route, part):
        for i in (5, 6, 7):
            reduced[route][i, part].wait_recv()
        span = SPANS[part]
        straight, cut = terms[route, 3 + c, span].astype(jnp.float32), terms[route, 4 - c, span].astype(jnp.float32)
        straight = straight + back[route, 5 + c, span].astype(jnp.float32) + back[route, 7, span].astype(jnp.float32)
        cut = cut + back[route, 6 - c, span].astype(jnp.float32)
        terms[route, 3 + c, span] = straight.astype(jnp.bfloat16)
        terms[route, 4 - c, span] = cut.astype(jnp.bfloat16)
        for i in (3, 4):
            add_up(route, i, along(route == 0, STEPS[i]), part)

    pairs = multiply(0)
    across = [cross(0, pairs)]
    pairs = multiply(1)
    across.append(cross(1, pairs))
    spread = [activate(g, across[g]) for g in range(2)]
    passed = [forward(g, spread[g]) for g in range(2)]
    for g in range(2):
        lower(g, passed[g])
    for part in (1, 0):
        for route in range(2):
            relay(route, part)

    early = len(sent)
    final = [[], []]
    for part in (1, 0):
        span = SPANS[part]
        for route in range(2):
            if part:
                for i in (1, 2):
                    reduced[route][i, 2].wait_recv()
            for i in (3, 4):
                reduced[route][i, part].wait_recv()
            added = terms[route, 0, span].astype(jnp.float32)
            for i in range(1, 5):
                added = added + back[route, i, span].astype(jnp.float32)
            onward[route, span] = added.astype(jnp.bfloat16)
            for i in ((3, 4, 1, 2), (7, 5, 6))[part]:
                final[route].append(
                    send(
                        onward.at[route, i],
                        last.at[route, i],
                        r2s.at[route, i],
                        r2r.at[route, i],
                        along(route == 1, STEPS[i]),
                    )
                )
    for copy in sent[:early]:
        copy.wait_send()
    sums = []
    for route in range(2):
        for copy in final[route]:
            copy.wait_recv()
        added = onward[route, 0].astype(jnp.float32)
        for i in range(1, N):
            added = added + last[route, i].astype(jnp.float32)
        sums.append(added)
    for half, part in enumerate(exchange(*sums)):
        lanes = slice(half * HALF, (half + 1) * HALF)
        out_ref[:, lanes] = (hidden_ref[:, lanes] + part).astype(jnp.bfloat16)
    for copy in sent[early:]:
        copy.wait_send()


def whole_layer(*operands):
    bf, f32 = jnp.bfloat16, jnp.float32
    dma = pltpu.SemaphoreType.DMA
    vmem = pltpu.VMEM
    return pl.pallas_call(
        kernel,
        out_shape=jax.ShapeDtypeStruct((8, 1024), bf),
        in_specs=[pl.BlockSpec(memory_space=pltpu.HBM)] * 11,
        out_specs=pl.BlockSpec(memory_space=vmem),
        scratch_shapes=[
            vmem((8, 1024), bf),
            vmem((8, 1024), bf),
            vmem((8, 512, 128), bf),
            vmem((8, 512, 128), bf),
            vmem((8, 128), bf),
            vmem((8, 128), bf),
            pltpu.SMEM((8,), jnp.int32),
            vmem((1024,), bf),
            vmem((64, 128), f32),
            vmem((8, 1024), f32),
            vmem((896, 1024), bf),
            vmem((UNITS, 1024), bf),
            vmem((2, N, N, 8, HALF), bf),
            vmem((2, N, N, 8, HALF), bf),
            vmem((2, N, N, 8, HALF), bf),
            vmem((2, N, 8, HALF), bf),
            vmem((2, N, 8, HALF), bf),
            dma((8,)),
            dma((4,)),
        ]
        + [dma((2, N))] * 2
        + [dma((2, 2, N))] * 4
        + [dma((2, N))] * 2
        + [
            shape
            for count in [len(places) for places in GROUPS]
            for shape in (
                vmem((N, count, 8, 1024), bf),
                vmem((N, 1, 128), f32),
                vmem((4, count, 8, 896), bf),
                vmem((4, count, 8, 896), bf),
                vmem((4, 1, 128), f32),
                vmem((4, count, 8, 896), f32),
                vmem((NX, count, 8, 896), bf),
                vmem((NX, count, 8, 896), bf),
                vmem((NX, 1, 128), f32),
                vmem((NX, 1, 128), f32),
                vmem((2 * NX, count, 8, UNITS), bf),
                dma((2,)),
                dma((2,)),
                dma((2, NX)),
                dma((2, NX)),
                dma((NX,)),
                dma((NX,)),
                dma((NX,)),
                dma((NX,)),
            )
        ],
        compiler_params=pltpu.CompilerParams(
            collective_id=0, has_side_effects=True, vmem_limit_bytes=60 * 1024 * 1024
        ),
        cost_estimate=pl.CostEstimate(flops=1_430_000_000, bytes_accessed=5_000_000, transcendentals=0),
        name="whole_layer",
    )(*operands)


def on_device(
    residual,
    queries,
    cache_keys,
    cache_values,
    new_keys,
    new_values,
    lengths,
    counts,
    norm_gain,
    gate_weight,
    up_weight,
    down_weight,
):
    result = whole_layer(
        residual,
        queries,
        cache_keys.reshape(8, 512, 128),
        cache_values.reshape(8, 512, 128),
        new_keys.reshape(8, 128),
        new_values.reshape(8, 128),
        lengths,
        norm_gain,
        gate_weight,
        up_weight,
        down_weight,
    )
    is_live = jnp.arange(8, dtype=jnp.int32) < counts[0]
    return jnp.where(is_live[:, None], result, jnp.zeros_like(result))


def solution(mesh):
    return jax.shard_map(
        on_device,
        mesh=mesh,
        in_specs=(
            P("attn", "ffn"),
            P("attn", "ffn"),
            P("attn", "ffn", None, None),
            P("attn", "ffn", None, None),
            P("attn", "ffn", None),
            P("attn", "ffn", None),
            P("attn"),
            P("attn"),
            P(),
            P("attn", "ffn"),
            P("attn", "ffn"),
            P("attn", "ffn"),
        ),
        out_specs=P("attn", "ffn"),
        check_vma=False,
    )
```

```python
import jax
import jax.numpy as jnp
from jax import lax
from jax.experimental import pallas as pl
from jax.experimental.pallas import tpu as pltpu
from jax.sharding import PartitionSpec as P

D = 8192


epsilon = 1e-05


MESH = pl.DeviceIdType.MESH
N = 8
NX = 4
HALF = 512
UNITS = 448
MAIN = 384
TILES = ((0, 256), (256, 256), (512, 256), (768, 128))
STEPS = (0, 1, -1, 2, -2, 3, -3, 4)
SPANS = (slice(0, 5), slice(5, 8), slice(0, 8))
GROUPS = ((0, 1, 2, 3, 4), (5, 6, 7))


def transposed_dot(rows, weight):
    return lax.dot_general(rows, weight, (((1,), (1,)), ((), ())), preferred_element_type=jnp.float32)


def exchange(low, high):
    axis = low.ndim - 2
    upper = lax.broadcasted_iota(jnp.int32, low.shape, axis) < 4
    return jnp.where(upper, low, pltpu.roll(high, 4, axis)), jnp.where(upper, pltpu.roll(low, 4, axis), high)


def attend(
    inputs,
    queries_ref,
    keys_ref,
    values_ref,
    new_keys_ref,
    new_values_ref,
    lengths_ref,
    residual_ref,
    by_head,
    hidden_ref,
):
    for load in inputs[:4]:
        load.wait()
    score_scale = 1.0 / 128**0.5
    for h in range(8):
        by_head[h * 8 : h * 8 + 8, :] = queries_ref[:, h * 128 : h * 128 + 128].astype(jnp.float32)
    new_keys = new_keys_ref[...].astype(jnp.float32)
    position = lax.broadcasted_iota(jnp.int32, (8, 512), 1)
    scores = []
    own = []
    for r in range(8):
        query = by_head[pl.ds(r, 8, stride=8), :]
        own.append(jnp.sum(query * new_keys[r : r + 1, :], axis=1, keepdims=True))
        slot = transposed_dot(query.astype(jnp.bfloat16), keys_ref[r]) * score_scale
        scores.append(jnp.where(position < lengths_ref[r], slot, -1e30))
    scores = jnp.concatenate(scores, axis=0)
    own = jnp.concatenate(own, axis=0) * score_scale
    row_max = jnp.maximum(jnp.max(scores, axis=1, keepdims=True), own)
    key_weights = jnp.exp(scores - row_max)
    own_weight = jnp.exp(own - row_max)
    denominator = jnp.sum(key_weights, axis=1, keepdims=True) + own_weight
    key_probs = key_weights / denominator
    own_prob = (own_weight / denominator).astype(jnp.bfloat16).astype(jnp.float32)
    for load in inputs[4:]:
        load.wait()
    new_values = new_values_ref[...].astype(jnp.float32)
    for r in range(8):
        probs = key_probs[r * 8 : r * 8 + 8, :].astype(jnp.bfloat16)
        mixed = jnp.dot(probs, values_ref[r], preferred_element_type=jnp.float32)
        mixed = mixed + own_prob[r * 8 : r * 8 + 8, :] * new_values[r : r + 1, :]
        by_head[pl.ds(r, 8, stride=8), :] = mixed.astype(jnp.bfloat16).astype(jnp.float32)
    for h in range(8):
        lanes = slice(h * 128, h * 128 + 128)
        hidden = residual_ref[:, lanes].astype(jnp.float32) + by_head[h * 8 : h * 8 + 8, :]
        hidden_ref[:, lanes] = hidden.astype(jnp.bfloat16).astype(jnp.float32)


def kernel(
    residual_hbm,
    queries_hbm,
    keys_hbm,
    values_hbm,
    new_keys_hbm,
    new_values_hbm,
    lengths_hbm,
    gain_hbm,
    gate_hbm,
    up_hbm,
    down_hbm,
    out_ref,
    residual_ref,
    queries_ref,
    keys_ref,
    values_ref,
    new_keys_ref,
    new_values_ref,
    lengths_ref,
    gain_ref,
    by_head,
    hidden_ref,
    gu,
    down,
    held,
    terms,
    back,
    onward,
    last,
    asem,
    wsem,
    g1s,
    g1r,
    g2s,
    g2r,
    r1s,
    r1r,
    r2s,
    r2r,
    *by_group,
):
    each = len(by_group) // len(GROUPS)
    by_group = [by_group[g * each : g * each + each] for g in range(len(GROUPS))]
    attn = lax.axis_index("attn")
    ffn = lax.axis_index("ffn")
    z, y = lax.div(attn, N), lax.rem(attn, N)
    x, c = lax.div(ffn, 2), lax.rem(ffn, 2)

    def at(zz, yy, xx, cc):
        return (zz * N + yy, xx * 2 + cc)

    def past(i, k, n):
        return lax.rem(i + k, n)

    inputs = [
        pltpu.make_async_copy(source, target, asem.at[i])
        for i, (source, target) in enumerate(
            (
                (queries_hbm, queries_ref),
                (new_keys_hbm, new_keys_ref),
                (lengths_hbm, lengths_ref),
                (keys_hbm, keys_ref),
                (values_hbm, values_ref),
                (new_values_hbm, new_values_ref),
                (residual_hbm, residual_ref),
                (gain_hbm.at[pl.ds(ffn * 1024, 1024)], gain_ref),
            )
        )
    ]
    for load in inputs:
        load.start()
    loads = [
        pltpu.make_async_copy(gate_hbm, gu.at[pl.ds(0, UNITS)], wsem.at[0]),
        pltpu.make_async_copy(up_hbm.at[pl.ds(MAIN, UNITS - MAIN)], gu.at[pl.ds(UNITS, UNITS - MAIN)], wsem.at[1]),
        pltpu.make_async_copy(up_hbm.at[pl.ds(0, MAIN)], gu.at[pl.ds(512, MAIN)], wsem.at[2]),
        pltpu.make_async_copy(down_hbm, down, wsem.at[3]),
    ]
    for load in loads:
        load.start()

    barrier = pltpu.get_barrier_semaphore()
    partners = [at(past(z, k, N), y, x, c) for k in range(1, N)]
    partners += [at(z, past(y, k, N), x, c) for k in range(1, N)]
    partners += [at(z, y, past(x, k, NX), core) for k in range(1, NX) for core in (c, 1 - c)]
    partners += [at(z, y, x, 1 - c)]
    for partner in partners:
        pl.semaphore_signal(barrier, inc=1, device_id=partner, device_id_type=MESH)

    attend(
        inputs,
        queries_ref,
        keys_ref,
        values_ref,
        new_keys_ref,
        new_values_ref,
        lengths_ref,
        residual_ref,
        by_head,
        hidden_ref,
    )
    gain = gain_ref[...].astype(jnp.float32).reshape(1, 1024)
    pl.semaphore_wait(barrier, len(partners))

    sent = []

    def send(source, target, send_sem, recv_sem, device):
        copy = pltpu.make_async_remote_copy(
            src_ref=source, dst_ref=target, send_sem=send_sem, recv_sem=recv_sem, device_id=device, device_id_type=MESH
        )
        copy.start()
        sent.append(copy)
        return copy

    other = at(z, y, x, 1 - c)

    def along(is_z, step):
        if is_z:
            return at(lax.rem(z + (N + step), N), y, x, c)
        return at(z, lax.rem(y + (N + step), N), x, c)

    blocks = exchange(hidden_ref[:, :HALF], hidden_ref[:, HALF:])
    first, second = [{}, {}], [{}, {}]
    for route in range(2):
        held[route, 0, 0] = blocks[route].astype(jnp.bfloat16)
    for i in (7, 5, 6, 3, 4, 1, 2):
        for route in range(2):
            first[route][i] = send(
                held.at[route, 0, 0],
                held.at[route, 0, i],
                g1s.at[route, i],
                g1r.at[route, i],
                along(route == 1, -STEPS[i]),
            )

    def pass_on(route, i, source, device, part):
        span = SPANS[part]
        second[route][i, part] = send(
            held.at[route, source, span],
            held.at[route, i, span],
            g2s.at[route, part % 2, i],
            g2r.at[route, part % 2, i],
            device,
        )

    for part, arrived in enumerate(((1, 2, 3, 4), (5, 6, 7))):
        for route in range(2):
            for i in arrived:
                first[route][i].wait_recv()
            for i in (3, 4):
                pass_on(route, i, 0, along(route == 0, -STEPS[i]), part)
    for route in range(2):
        for i in (1, 2):
            pass_on(route, i, 0, along(route == 0, -STEPS[i]), 2)
    for part in range(2):
        for route in range(2):
            second[route][3, part].wait_recv()
            second[route][4, part].wait_recv()
            pass_on(route, 7, 3 + c, along(route == 0, -2 + 4 * c), part)
            pass_on(route, 5, 3, along(route == 0, -1), part)
            pass_on(route, 6, 4, along(route == 0, 1), part)

    def multiply(g):
        xs, ssb, pair_out, pair_in, pair_ss, own = by_group[g][:6]
        places = GROUPS[g]
        count = len(places)
        lane = lax.broadcasted_iota(jnp.int32, (4, 8, 128), 2)
        row = lax.broadcasted_iota(jnp.int32, (4, 8, 128), 1)
        for route in range(2):
            squares = jnp.zeros((4, 1, 128), jnp.float32)
            for d, i in enumerate(places):
                for part in {1: (2,), 2: (2,), 5: (0, 1), 6: (0, 1), 7: (0, 1)}.get(i, ()):
                    second[route][i, part].wait_recv()
                packed = held[route, i].astype(jnp.float32).reshape(4, 2, 8, HALF)
                low, high = exchange(packed[:, 0], packed[:, 1])
                square = jnp.sum(low * low + high * high, axis=2, keepdims=True)
                squares = squares + jnp.sum(jnp.where(lane == row + 8 * d, square, 0.0), axis=1, keepdims=True)
                xs[route * 4 : route * 4 + 4, d, :, :HALF] = (low * gain[:, :HALF]).astype(jnp.bfloat16)
                xs[route * 4 : route * 4 + 4, d, :, HALF:] = (high * gain[:, HALF:]).astype(jnp.bfloat16)
            ssb[route * 4 : route * 4 + 4] = squares
        if g == 0:
            for load in loads:
                load.wait()
        rows = xs[pl.ds((1 - c) * 4, 4)].reshape(32 * count, 1024)
        for start, width in TILES:
            block = transposed_dot(rows, gu[start : start + width, :]).astype(jnp.bfloat16)
            pair_out[:, :, :, start : start + width] = block.reshape(4, count, 8, width)
        pair = [
            send(pair_out, pair_in, by_group[g][11].at[0], by_group[g][12].at[0], other),
            send(ssb.at[pl.ds((1 - c) * 4, 4)], pair_ss, by_group[g][11].at[1], by_group[g][12].at[1], other),
        ]
        rows = xs[pl.ds(c * 4, 4)].reshape(32 * count, 1024)
        for start, width in TILES:
            block = transposed_dot(rows, gu[start : start + width, :])
            own[:, :, :, start : start + width] = block.reshape(4, count, 8, width)
        return pair

    def cross(g, before):
        ssb, _, pair_in, pair_ss, own, x_out, x_in, x_ss_out, x_ss_in = by_group[g][1:10]
        xss, xsr = by_group[g][13:15]
        for copy in before:
            copy.wait_recv()
        copies = []
        for k in (2, 1, 3):
            xx = past(x, k, NX)
            x_out[k] = (own[xx] + pair_in[xx].astype(jnp.float32)).astype(jnp.bfloat16)
            x_ss_out[k] = ssb[c * 4 + xx] + pair_ss[xx]
            device = at(z, y, xx, c)
            copies.append(send(x_out.at[k], x_in.at[k], xss.at[0, k], xsr.at[0, k], device))
            copies.append(send(x_ss_out.at[k], x_ss_in.at[k], xss.at[1, k], xsr.at[1, k], device))
        return copies

    def activate(g, before):
        ssb, _, pair_in, pair_ss, own, _, x_in, _, x_ss_in, act = by_group[g][1:11]
        acs, acr, fws, fwr = by_group[g][15:19]
        count = len(GROUPS[g])
        total = own[x] + pair_in[x].astype(jnp.float32)
        squares = ssb[c * 4 + x] + pair_ss[x]
        for copy in before:
            copy.wait_recv()
        for k in range(1, NX):
            total = total + x_in[k].astype(jnp.float32)
            squares = squares + x_ss_in[k]
        total = total.reshape(8 * count, 896)
        lane = lax.broadcasted_iota(jnp.int32, (8 * count, 128), 1)
        row = lax.broadcasted_iota(jnp.int32, (8 * count, 128), 0)
        mean_square = jnp.sum(jnp.where(lane == row, squares, 0.0), axis=1, keepdims=True) / D
        total = total * lax.rsqrt(mean_square + epsilon)
        gate = total[:, :512]
        silu = gate / (1.0 + jnp.exp(-gate))
        mine = c * 4 + x
        main = (silu[:, :MAIN] * total[:, 512:]).astype(jnp.bfloat16)
        act[mine, :, :, :MAIN] = main.reshape(count, 8, MAIN)
        tail = (silu[:, MAIN:] * pltpu.roll(total[:, MAIN:512], 64, 1))[:, : UNITS - MAIN]
        act[mine, :, :, MAIN:] = tail.astype(jnp.bfloat16).reshape(count, 8, UNITS - MAIN)
        copies = []
        for k in (2, 1, 3):
            device = at(z, y, past(x, k, NX), c)
            copies.append(send(act.at[mine], act.at[mine], acs.at[k], acr.at[k], device))
        passed = [send(act.at[mine], act.at[mine], fws.at[0], fwr.at[0], other)]
        if g == 1:
            for k in (2, 1, 3):
                device = at(z, y, past(x, k, NX), 1 - c)
                passed.append(send(act.at[mine], act.at[mine], fws.at[k], fwr.at[k], device))
        return copies, passed

    def forward(g, before):
        act = by_group[g][10]
        fws, fwr = by_group[g][17:19]
        copies, passed = before
        if g == 1:
            return copies + passed
        for k, copy in zip((1, 3, 2), (copies[1], copies[2], copies[0])):
            copy.wait_recv()
            place = c * 4 + past(x, NX - k, NX)
            passed.append(send(act.at[place], act.at[place], fws.at[k], fwr.at[k], other))
        return passed

    reduced = [{}, {}]

    def lower(g, before):
        act = by_group[g][10]
        places = GROUPS[g]
        count = len(places)
        for copy in before:
            copy.wait_recv()
        rows = act[...].reshape(64 * count, UNITS)
        for start in (0, 256):
            quarters = [
                jnp.dot(rows, down[:, at_lane : at_lane + 256], preferred_element_type=jnp.float32)
                for at_lane in (start, start + HALF)
            ]
            halves = exchange(*[quarter.reshape(2, 4, count, 8, 256) for quarter in quarters])
            for route in range(2):
                for d, i in enumerate(places):
                    block = jnp.stack([half[route, :, d] for half in halves], axis=1)
                    terms[route, i, :, :, start : start + 256] = block.reshape(N, 8, 256).astype(jnp.bfloat16)
        for part in (2,) if g == 0 else (1, 0):
            for i in (1, 2) if g == 0 else (7, 5, 6):
                for route in range(2):
                    step = {1: 1, 2: -1, 5: 1, 6: -1, 7: 2 - 4 * c}[i]
                    add_up(route, i, along(route == 0, step), part)

    def add_up(route, i, device, part):
        reduced[route][i, part] = send(
            terms.at[route, i, SPANS[part]],
            back.at[route, i, SPANS[part]],
            r1s.at[part % 2, route, i],
            r1r.at[part % 2, route, i],
            device,
        )

    def relay(route, part):
        for i in (5, 6, 7):
            reduced[route][i, part].wait_recv()
        span = SPANS[part]
        straight, cut = terms[route, 3 + c, span].astype(jnp.float32), terms[route, 4 - c, span].astype(jnp.float32)
        straight = straight + back[route, 5 + c, span].astype(jnp.float32) + back[route, 7, span].astype(jnp.float32)
        cut = cut + back[route, 6 - c, span].astype(jnp.float32)
        terms[route, 3 + c, span] = straight.astype(jnp.bfloat16)
        terms[route, 4 - c, span] = cut.astype(jnp.bfloat16)
        for i in (3, 4):
            add_up(route, i, along(route == 0, STEPS[i]), part)

    pairs = multiply(0)
    across = [cross(0, pairs)]
    pairs = multiply(1)
    across.append(cross(1, pairs))
    spread = [activate(g, across[g]) for g in range(2)]
    passed = [forward(g, spread[g]) for g in range(2)]
    for g in range(2):
        lower(g, passed[g])
    for part in (1, 0):
        for route in range(2):
            relay(route, part)

    early = len(sent)
    final = [[], []]
    for part in (1, 0):
        span = SPANS[part]
        for route in range(2):
            if part:
                for i in (1, 2):
                    reduced[route][i, 2].wait_recv()
            for i in (3, 4):
                reduced[route][i, part].wait_recv()
            added = terms[route, 0, span].astype(jnp.float32)
            for i in range(1, 5):
                added = added + back[route, i, span].astype(jnp.float32)
            onward[route, span] = added.astype(jnp.bfloat16)
            for i in ((3, 4, 1, 2), (7, 5, 6))[part]:
                final[route].append(
                    send(
                        onward.at[route, i],
                        last.at[route, i],
                        r2s.at[route, i],
                        r2r.at[route, i],
                        along(route == 1, STEPS[i]),
                    )
                )
    for copy in sent[:early]:
        copy.wait_send()
    sums = []
    for route in range(2):
        for copy in final[route]:
            copy.wait_recv()
        added = onward[route, 0].astype(jnp.float32)
        for i in range(1, N):
            added = added + last[route, i].astype(jnp.float32)
        sums.append(added)
    for half, part in enumerate(exchange(*sums)):
        lanes = slice(half * HALF, (half + 1) * HALF)
        out_ref[:, lanes] = (hidden_ref[:, lanes] + part).astype(jnp.bfloat16)
    for copy in sent[early:]:
        copy.wait_send()


def whole_layer(*operands):
    bf, f32 = jnp.bfloat16, jnp.float32
    dma = pltpu.SemaphoreType.DMA
    vmem = pltpu.VMEM
    return pl.pallas_call(
        kernel,
        out_shape=jax.ShapeDtypeStruct((8, 1024), bf),
        in_specs=[pl.BlockSpec(memory_space=pltpu.HBM)] * 11,
        out_specs=pl.BlockSpec(memory_space=vmem),
        scratch_shapes=[
            vmem((8, 1024), bf),
            vmem((8, 1024), bf),
            vmem((8, 512, 128), bf),
            vmem((8, 512, 128), bf),
            vmem((8, 128), bf),
            vmem((8, 128), bf),
            pltpu.SMEM((8,), jnp.int32),
            vmem((1024,), bf),
            vmem((64, 128), f32),
            vmem((8, 1024), f32),
            vmem((896, 1024), bf),
            vmem((UNITS, 1024), bf),
            vmem((2, N, N, 8, HALF), bf),
            vmem((2, N, N, 8, HALF), bf),
            vmem((2, N, N, 8, HALF), bf),
            vmem((2, N, 8, HALF), bf),
            vmem((2, N, 8, HALF), bf),
            dma((8,)),
            dma((4,)),
        ]
        + [dma((2, N))] * 2
        + [dma((2, 2, N))] * 4
        + [dma((2, N))] * 2
        + [
            shape
            for count in [len(places) for places in GROUPS]
            for shape in (
                vmem((N, count, 8, 1024), bf),
                vmem((N, 1, 128), f32),
                vmem((4, count, 8, 896), bf),
                vmem((4, count, 8, 896), bf),
                vmem((4, 1, 128), f32),
                vmem((4, count, 8, 896), f32),
                vmem((NX, count, 8, 896), bf),
                vmem((NX, count, 8, 896), bf),
                vmem((NX, 1, 128), f32),
                vmem((NX, 1, 128), f32),
                vmem((2 * NX, count, 8, UNITS), bf),
                dma((2,)),
                dma((2,)),
                dma((2, NX)),
                dma((2, NX)),
                dma((NX,)),
                dma((NX,)),
                dma((NX,)),
                dma((NX,)),
            )
        ],
        compiler_params=pltpu.CompilerParams(
            collective_id=0, has_side_effects=True, vmem_limit_bytes=(53 * 1024 + 924) * 1024
        ),
        cost_estimate=pl.CostEstimate(flops=1_430_000_000, bytes_accessed=5_000_000, transcendentals=0),
        name="whole_layer",
    )(*operands)


def on_device(
    residual,
    queries,
    cache_keys,
    cache_values,
    new_keys,
    new_values,
    lengths,
    counts,
    norm_gain,
    gate_weight,
    up_weight,
    down_weight,
):
    result = whole_layer(
        residual,
        queries,
        cache_keys.reshape(8, 512, 128),
        cache_values.reshape(8, 512, 128),
        new_keys.reshape(8, 128),
        new_values.reshape(8, 128),
        lengths,
        norm_gain,
        gate_weight,
        up_weight,
        down_weight,
    )
    is_live = jnp.arange(8, dtype=jnp.int32) < counts[0]
    return jnp.where(is_live[:, None], result, jnp.zeros_like(result))


def solution(mesh):
    return jax.shard_map(
        on_device,
        mesh=mesh,
        in_specs=(
            P("attn", "ffn"),
            P("attn", "ffn"),
            P("attn", "ffn", None, None),
            P("attn", "ffn", None, None),
            P("attn", "ffn", None),
            P("attn", "ffn", None),
            P("attn"),
            P("attn"),
            P(),
            P("attn", "ffn"),
            P("attn", "ffn"),
            P("attn", "ffn"),
        ),
        out_specs=P("attn", "ffn"),
        check_vma=False,
    )
```
